256 devices in a mesh: target: 8 (over x, core), context: 16 (over z_lo, y), offset: 2 (over z_hi).
Axes of the slice: x: 4, y: 4, z: 8 (z_hi: 2, z_lo: 4; z = z_hi * 4 + z_lo), core: 2. Of those that a mesh axis runs over, the one named last changes fastest.
Arguments:
- tensor: bfloat16 [64, 8192, 2048], P('offset', 'target', 'context'), may hold values from -6 to 6
- context_factor: bfloat16 [2048, 256], P('context'), may hold values from -0.125 to 0.125
- offset_factor: bfloat16 [64, 8], P('offset'), may hold values from -0.75 to 0.75
- target_factor: bfloat16 [8192, 256], P('target'), may hold values from -6 to 6
Outputs:
- new_factor: float32 [8192, 256], P('target')
The draws below stay inside these ranges and needn't reach their ends.
All inputs are finite; a program needn't handle non-finite values.
Results may differ from the reference program's by a relative error of at most 0.0003.
Values sent between devices are 32-bit elements; how exact they have to be, the bound alone decides.
No kernel may reach another device: no remote copies, remote signals or barrier semaphores. Data moves between devices by JAX's collectives and lax.ppermute only.
A program may use at most 128 MiB of HBM per device.

```python
import jax
import jax.numpy as jnp
from jax import lax

R1 = 256
R2 = 256
R3 = 8
K = 64
I = 8192
J = 2048


def block_scale(own_key, dims, split, least, top_value):
    loudness, own = 1.0, jax.random.fold_in(own_key, 6)
    for axis_at, blocks in split:
        steps = jnp.exp(jax.random.uniform(jax.random.fold_in(own, axis_at), (blocks,), jnp.float32, least / len(split), top_value / len(split)))
        loudness = loudness * jnp.repeat(steps, dims[axis_at] // blocks).reshape([-1 if axis == axis_at else 1 for axis in range(len(dims))])
    return loudness


def noise(own_key, dims, spread, limit, shards=(), held_as=jnp.bfloat16):
    values = jax.random.normal(own_key, dims, jnp.float32) * spread
    if len(shards) > 0:
        values = block_scale(own_key, dims, shards, -0.22, 0.18) * values
    return jnp.clip(values, min=-limit, max=limit).astype(held_as)


def setup_inputs(seed: int = 0) -> dict:
    streams_of = jax.random.split(jax.random.key(seed), 5)
    return {
        "tensor": noise(streams_of[0], (K, I, J), 1.0, 6.0, ((0, 2), (1, 8), (2, 16))),
        "context_factor": noise(streams_of[1], (J, R2), J ** -0.5, 0.125, ((0, 16),)),
        "offset_factor": noise(streams_of[2], (K, R3), K ** -0.5, 0.75, ((0, 2),)),
        "target_factor": noise(streams_of[3], (I, R1), 1.0, 6.0, ((0, 8),)),
    }


def reference(tensor, context_factor, offset_factor, target_factor):
    highest = lax.Precision.HIGHEST

    def add_offset(total, pair):
        block, coeffs = pair
        partial_value = jnp.dot(block.astype(jnp.float32), context_factor.astype(jnp.float32), preferred_element_type=jnp.float32)
        term = coeffs.astype(jnp.float32)[None, :, None] * partial_value[:, None, :]
        return (total + term, None)
    start = jnp.zeros((tensor.shape[1], offset_factor.shape[1], context_factor.shape[1]), jnp.float32)
    core, unused = lax.scan(add_offset, start, (tensor, offset_factor))
    core = core.reshape(core.shape[0], -1)
    factor = target_factor.astype(jnp.float32)
    weights = jnp.dot(core.T, factor, precision=highest)
    basis = jnp.dot(core, weights, precision=highest)
    gram = jnp.dot(basis.T, basis, precision=highest) / basis.shape[0]
    lower = jnp.linalg.cholesky(gram)
    return jax.scipy.linalg.solve_triangular(lower, basis.T, lower=True).T
```

```python
import functools

import jax
import jax.numpy as jnp
from jax import lax
from jax.experimental import pallas as pl
from jax.experimental.pallas import tpu as pltpu
from jax.sharding import Mesh
from jax.sharding import PartitionSpec as P

F32, BF16 = jnp.float32, jnp.bfloat16
TARGET = ("x", "core")
GROUP = ("zlo", "y", "zhi")
RING = ("zhi", "zlo")
ROWS_AT_ONCE = 256
NN = (((1,), (0,)), ((), ()))
TN = (((0,), (0,)), ((), ()))
NT = (((1,), (1,)), ((), ()))


def mm(a, b, dims=NN):
    return lax.dot_general(a, b, dims, preferred_element_type=F32)


def halves(value):
    high = value.astype(BF16)
    return high, (value - high.astype(F32)).astype(BF16)


def thirds(value):
    high = value.astype(BF16)
    rest = value - high.astype(F32)
    middle = rest.astype(BF16)
    return high, middle, (rest - middle.astype(F32)).astype(BF16)


def call(kernel, out_shape, **more):
    return pl.pallas_call(
        kernel,
        out_shape=out_shape,
        compiler_params=pltpu.CompilerParams(vmem_limit_bytes=48 * 2**20),
        **more,
    )


def project_kernel(spread_ref, factor_ref, tensor_ref, high_ref, low_ref, out_ref):
    spread = spread_ref[...]
    ranks = spread.shape[0] // 16
    width = tensor_ref.shape[2]
    for at in range(0, tensor_ref.shape[1], 32):
        sides = [
            tensor_ref[:, at + half : at + half + 16, :].reshape(-1, width) for half in (0, 16)
        ]
        high, low = halves(mm(spread, jnp.concatenate(sides, axis=1)))
        for rank in range(ranks):
            to = slice(rank * width, (rank + 1) * width)
            of = slice(rank * 16, rank * 16 + 16)
            for side in (0, 1):
                rows = slice(at + 16 * side, at + 16 * side + 16)
                lanes = slice(side * width, (side + 1) * width)
                high_ref[rows, to] = high[of, lanes]
                low_ref[rows, to] = low[of, lanes]

    @pl.when(pl.program_id(0) == 0)
    def _():
        out_ref[...] = jnp.zeros_like(out_ref)

    factor = factor_ref[...]
    for rank in range(ranks):
        to = slice(rank * width, (rank + 1) * width)
        out_ref[rank] += mm(factor, high_ref[:, to]) + mm(factor, low_ref[:, to])


def project(tensor, spread, factor_t):
    offsets, rows, width = tensor.shape
    ranks = spread.shape[0] // 16
    wide = ranks * width
    return call(
        project_kernel,
        (
            jax.ShapeDtypeStruct((rows, wide), BF16),
            jax.ShapeDtypeStruct((rows, wide), BF16),
            jax.ShapeDtypeStruct((ranks, factor_t.shape[0], width), F32),
        ),
        grid=(rows // ROWS_AT_ONCE,),
        in_specs=[
            pl.BlockSpec(spread.shape, lambda i: (0, 0)),
            pl.BlockSpec((factor_t.shape[0], ROWS_AT_ONCE), lambda i: (0, i)),
            pl.BlockSpec((offsets, ROWS_AT_ONCE, width), lambda i: (0, i, 0)),
        ],
        out_specs=(
            pl.BlockSpec((ROWS_AT_ONCE, wide), lambda i: (i, 0)),
            pl.BlockSpec((ROWS_AT_ONCE, wide), lambda i: (i, 0)),
            pl.BlockSpec((ranks, factor_t.shape[0], width), lambda i: (0, 0, 0)),
        ),
    )(spread, factor_t, tensor)


def weights_kernel(parts_ref, context_ref, out_ref):
    high, low = halves(jnp.sum(parts_ref[...], axis=0))
    context = context_ref[...]
    out_ref[...] = mm(high, context) + mm(low, context)


def sum_and_copy_kernel(parts_ref, out_ref):
    out_ref[...] = jnp.broadcast_to(jnp.sum(parts_ref[...], axis=0)[None], out_ref.shape)


def expand_kernel(weights_ref, context_ref, out_ref):
    high, low = halves(weights_ref[...])
    context = context_ref[...]
    value = mm(context, high, NT) + mm(context, low, NT)
    out_ref[...] = jnp.broadcast_to(value[None], out_ref.shape)


def basis_kernel(high_ref, low_ref, own_ref, other_ref, out_ref, vhigh_ref, vlow_ref):
    @pl.when(pl.program_id(0) == 0)
    def _():
        depth = own_ref.shape[0]
        for at, ref in ((0, own_ref), (depth, other_ref)):
            high, low = halves(ref[...])
            vhigh_ref[at : at + depth, :] = high
            vlow_ref[at : at + depth, :] = low

    high, vhigh = high_ref[...], vhigh_ref[...]
    out_ref[...] = mm(high, vhigh) + (mm(high, vlow_ref[...]) + mm(low_ref[...], vhigh))


def make_basis(high, low, own, other):
    rows, wide = high.shape
    columns = own.shape[1]
    return call(
        basis_kernel,
        jax.ShapeDtypeStruct((rows, columns), F32),
        grid=(rows // ROWS_AT_ONCE,),
        in_specs=[
            pl.BlockSpec((ROWS_AT_ONCE, wide), lambda i: (i, 0)),
            pl.BlockSpec((ROWS_AT_ONCE, wide), lambda i: (i, 0)),
            pl.BlockSpec(own.shape, lambda i: (0, 0)),
            pl.BlockSpec(own.shape, lambda i: (0, 0)),
        ],
        out_specs=pl.BlockSpec((ROWS_AT_ONCE, columns), lambda i: (i, 0)),
        scratch_shapes=[pltpu.VMEM((wide, columns), BF16)] * 2,
    )(high, low, own, other)


def gram_kernel(basis_ref, out_ref):
    high, low = halves(basis_ref[...])
    cross = mm(high, low, TN)
    out_ref[...] = mm(high, high, TN) + (cross + cross.T)


def row(value, at):
    return jnp.broadcast_to(value[at : at + 1, :], value.shape)


def small_inverse(block):
    shape = (8, 128)
    at_row = lax.broadcasted_iota(jnp.int32, shape, 0)
    left = [jnp.broadcast_to(block[:, k : k + 1], shape) for k in range(8)]
    right = [(at_row == k).astype(F32) for k in range(8)]
    scale = jnp.zeros(shape, F32)
    for j in range(8):
        pivot = row(left[j], j)
        scale = jnp.where(at_row == j, lax.rsqrt(pivot), scale)
        if j < 7:
            ratio = jnp.where(at_row > j, left[j] / pivot, 0.0)
            for k in range(j + 1, 8):
                left[k] = left[k] - ratio * row(left[k], j)
            for k in range(j + 1):
                right[k] = right[k] - ratio * row(right[k], j)
    return [value * scale for value in right]


def inverse_factor(work_ref):
    size = work_ref.shape[0]
    for top in range(0, size, 32):
        tiles = list(range(top // 128, size // 128))
        tiles += [size // 128 + t for t in range(top // 128 + 1)]
        rows = [
            {t: work_ref[top + 8 * q : top + 8 * q + 8, 128 * t : 128 * t + 128] for t in tiles}
            for q in range(4)
        ]
        for q in range(4):
            first = top + 8 * q
            tile, lane = first // 128, first % 128
            inverse = small_inverse(rows[q][tile][:, lane : lane + 8])
            mine = {}
            for t in tiles:
                mine[t] = sum(inverse[k] * row(rows[q][t], k) for k in range(8))
            rows[q] = mine
            if q < 3:
                coeffs = {(m, k): row(inverse[k], m) for m in range(8) for k in range(m + 1)}
            for other in range(q + 1, 4):
                column = [
                    jnp.broadcast_to(rows[other][tile][:, lane + k : lane + k + 1], (8, 128))
                    for k in range(8)
                ]
                factor = [sum(column[k] * coeffs[m, k] for k in range(m + 1)) for m in range(8)]
                for t in tiles:
                    rows[other][t] = rows[other][t] - sum(factor[m] * row(mine[t], m) for m in range(8))
        for q in range(4):
            for t in tiles:
                work_ref[top + 8 * q : top + 8 * q + 8, 128 * t : 128 * t + 128] = rows[q][t]
        below = top + 32
        if below < size:
            done = jnp.concatenate(
                [jnp.concatenate([rows[q][t] for q in range(4)], axis=0) for t in tiles], axis=1
            )
            high, middle, low = thirds(done)
            left = jnp.concatenate([high, high, middle, high, low, middle], axis=0)
            right = jnp.concatenate([high, middle, high, low, high, middle], axis=0)
            start = 128 * tiles[0]
            skip = below % 128
            change = mm(left[:, below - skip - start : size - start], right, TN)
            for n, t in enumerate(tiles):
                work_ref[below:, 128 * t : 128 * t + 128] -= change[skip:, 128 * n : 128 * n + 128]


def finish_kernel(rows_total, basis_ref, own_ref, other_ref, core_ref, out_ref, work_ref):
    size = basis_ref.shape[1]
    own, other = own_ref[...] / rows_total, other_ref[...] / rows_total
    flip = core_ref[0] != 0
    half = size // 2
    work_ref[:half, :size] = jnp.where(flip, other, own)
    work_ref[half:, :size] = jnp.where(flip, own, other)
    at_row = lax.broadcasted_iota(jnp.int32, (size, size), 0)
    at_column = lax.broadcasted_iota(jnp.int32, (size, size), 1)
    work_ref[:, size:] = (at_row == at_column).astype(F32)
    inverse_factor(work_ref)
    at_row = lax.broadcasted_iota(jnp.int32, (size, size), 0)
    at_column = lax.broadcasted_iota(jnp.int32, (size, size), 1)
    ihigh, ilow = halves(jnp.where(at_row >= at_column, work_ref[:, size:], 0.0))
    high, low = halves(basis_ref[...])
    out_ref[...] = mm(high, ihigh, NT) + (mm(high, ilow, NT) + mm(low, ihigh, NT))


def everyone(value, axes):
    return lax.all_to_all(value, axes, 0, 0)


def copies(value, number):
    return jnp.broadcast_to(value[None], (number,) + value.shape)


def swap(value):
    return lax.ppermute(value, "core", [(0, 1), (1, 0)])


def on_device(tensor, context, offset, target):
    offsets, rows, width = tensor.shape
    ranks, columns = offset.shape[1], target.shape[1]
    nx, ny, nz = lax.axis_size("x"), lax.axis_size("y"), lax.axis_size(RING)
    core = lax.axis_index("core")
    flip = core != 0

    pairs = offset.reshape(offsets, ranks // 2, 2)
    pairs = jnp.where(flip, pairs[..., ::-1], pairs)
    ordered = pairs.transpose(2, 1, 0).reshape(ranks, offsets)
    eye = jnp.eye(16, dtype=BF16)
    spread = (ordered[:, None, :, None] * eye[None, :, None, :]).reshape(ranks * 16, offsets * 16)
    high, low, product = project(tensor, spread, target.T)

    half = ranks // 2
    product = product[:half] + swap(product[half:])
    product = everyone(product, "x")
    part = call(weights_kernel, jax.ShapeDtypeStruct((columns, context.shape[1]), F32))(product, context)
    size = ny * nz
    part = everyone(part.reshape(size, columns // size, -1), GROUP)
    part = call(sum_and_copy_kernel, jax.ShapeDtypeStruct(part.shape, F32))(part)
    weights = everyone(part, GROUP).reshape(columns, -1)
    expanded = call(expand_kernel, jax.ShapeDtypeStruct((nx, width, columns), F32))(weights, context)
    own = everyone(expanded, "x").reshape(half * width, columns)
    basis = make_basis(high, low, own, swap(own))

    basis = jnp.sum(everyone(basis.reshape(ny, rows // ny, columns), "y"), axis=0)
    basis = everyone(basis.reshape(nz, rows // ny // nz, columns), RING)
    basis = call(sum_and_copy_kernel, jax.ShapeDtypeStruct(basis.shape, F32))(basis)
    basis = everyone(basis, RING).reshape(rows // ny, columns)
    basis = everyone(copies(basis, ny), "y").reshape(rows, columns)

    gram = call(gram_kernel, jax.ShapeDtypeStruct((columns, columns), F32))(basis)
    gram = gram + swap(gram)
    side = columns // 2
    mine = jnp.where(flip, gram[side:], gram[:side])
    mine = jnp.sum(everyone(copies(mine, nx), "x"), axis=0)
    return call(
        functools.partial(finish_kernel, rows * lax.axis_size(TARGET)),
        jax.ShapeDtypeStruct((rows, columns), F32),
        in_specs=[pl.BlockSpec(memory_space=pltpu.VMEM)] * 3 + [pl.BlockSpec(memory_space=pltpu.SMEM)],
        scratch_shapes=[pltpu.VMEM((columns, 2 * columns), F32)],
    )(basis, mine, swap(mine), core.reshape(1).astype(jnp.int32))


def solution(mesh):
    fine = Mesh(mesh.devices.reshape(4, 2, 4, 4, 2), ("x", "core") + GROUP)
    placed = (
        P("zhi", TARGET, ("zlo", "y")),
        P(("zlo", "y"), None),
        P("zhi", None),
        P(TARGET, None),
    )
    return jax.shard_map(
        on_device, mesh=fine, in_specs=placed, out_specs=P(TARGET, None), check_vma=False
    )
```

```python
import functools

import jax
import jax.numpy as jnp
from jax import lax
from jax.experimental import pallas as pl
from jax.experimental.pallas import tpu as pltpu
from jax.sharding import Mesh
from jax.sharding import PartitionSpec as P

F32, BF16 = jnp.float32, jnp.bfloat16
TARGET = ("x", "core")
GROUP = ("zlo", "y", "zhi")
RING = ("zhi", "zlo")
ROWS_AT_ONCE = 256
NN = (((1,), (0,)), ((), ()))
TN = (((0,), (0,)), ((), ()))
NT = (((1,), (1,)), ((), ()))


def mm(a, b, dims=NN):
    return lax.dot_general(a, b, dims, preferred_element_type=F32)


def halves(value):
    high = value.astype(BF16)
    return high, (value - high.astype(F32)).astype(BF16)


def thirds(value):
    high = value.astype(BF16)
    rest = value - high.astype(F32)
    middle = rest.astype(BF16)
    return high, middle, (rest - middle.astype(F32)).astype(BF16)


VMEM_SPEC = pl.BlockSpec(memory_space=pltpu.VMEM)


def in_hbm(value):
    return pltpu.with_memory_space_constraint(value, pltpu.HBM)


def in_vmem(value):
    return pltpu.with_memory_space_constraint(value, pltpu.VMEM)


def call(kernel, out_shape, vmem=16, **more):
    return pl.pallas_call(
        kernel,
        out_shape=out_shape,
        compiler_params=pltpu.CompilerParams(vmem_limit_bytes=vmem * 2**20),
        **more,
    )


def project_kernel(
    core_ref,
    offset_hbm,
    target_hbm,
    tensor_ref,
    high_ref,
    low_hbm,
    out_ref,
    low_ref,
    held_ref,
    offset_ref,
    target_ref,
    factor_ref,
    sems,
):
    offsets, rows, width = tensor_ref.shape
    ranks = offset_ref.shape[0]
    blocks = held_ref.shape[0]
    depth = held_ref.shape[2]
    small = [
        pltpu.make_async_copy(offset_hbm, offset_ref, sems.at[blocks]),
        pltpu.make_async_copy(target_hbm, target_ref, sems.at[blocks + 1]),
    ]
    for copy in small:
        copy.start()
    for block in range(blocks):
        pltpu.make_async_copy(
            tensor_ref.at[:, pl.ds(block * depth, depth), :], held_ref.at[block], sems.at[block]
        ).start()
    for copy in small:
        copy.wait()

    def iota(shape, dim):
        return lax.broadcasted_iota(jnp.int32, shape, dim)

    tall, wide = (ranks * 16, ranks), (offsets, offsets * 16)
    place = iota(tall, 0) // 16
    half = ranks // 2
    rank_at = 2 * (place % half) + jnp.where(place >= half, 1 - core_ref[0], core_ref[0])
    pick = (rank_at == iota(tall, 1)).astype(BF16)
    repeat = (iota(wide, 0) == iota(wide, 1) // 16).astype(BF16)
    spread = mm(mm(pick, offset_ref[...]).astype(BF16), repeat)
    same = iota(spread.shape, 0) % 16 == iota(spread.shape, 1) % 16
    spread = jnp.where(same, spread, 0.0).astype(BF16)
    factor_ref[...] = target_ref[...].astype(F32).T.astype(BF16)

    def contract(block):
        base = block * depth
        for at in range(0, depth, 32):
            sides = [
                held_ref[block, :, at + side : at + side + 16, :].reshape(-1, width) for side in (0, 16)
            ]
            high, low = halves(mm(spread, jnp.concatenate(sides, axis=1)))
            for rank in range(ranks):
                to = slice(rank * width, (rank + 1) * width)
                of = slice(rank * 16, rank * 16 + 16)
                for side in (0, 1):
                    rows_at = slice(base + at + 16 * side, base + at + 16 * side + 16)
                    lanes = slice(side * width, (side + 1) * width)
                    high_ref[rows_at, to] = high[of, lanes]
                    low_ref[rows_at, to] = low[of, lanes]

    def add_product(block):
        here = slice(block * depth, (block + 1) * depth)
        factor = factor_ref[:, here]
        for rank in range(0, ranks, 2):
            to = slice(rank * width, (rank + 2) * width)
            change = mm(factor, high_ref[here, to]) + mm(factor, low_ref[here, to])
            for side in (0, 1):
                part = change[:, side * width : (side + 1) * width]
                out_ref[rank + side] = part if block == 0 else out_ref[rank + side] + part

    def keep(block):
        here = pl.ds(block * depth, depth)
        return pltpu.make_async_copy(low_ref.at[here, :], low_hbm.at[here, :], sems.at[blocks + 2 + block])

    for block in range(blocks):
        pltpu.make_async_copy(
            tensor_ref.at[:, pl.ds(block * depth, depth), :], held_ref.at[block], sems.at[block]
        ).wait()
        contract(block)
        if block > 0:
            add_product(block - 1)
        keep(block).start()
    add_product(blocks - 1)
    for block in range(blocks):
        keep(block).wait()


def project(core, offset, target, tensor):
    offsets, rows, width = tensor.shape
    ranks, columns = offset.shape[1], target.shape[1]
    wide = ranks * width
    blocks = rows // ROWS_AT_ONCE
    return call(
        project_kernel,
        (
            jax.ShapeDtypeStruct((rows, wide), BF16),
            pltpu.HBM((rows, wide), BF16),
            jax.ShapeDtypeStruct((ranks, columns, width), F32),
        ),
        vmem=24,
        in_specs=[
            pl.BlockSpec(memory_space=pltpu.SMEM),
        ]
        + [pl.BlockSpec(memory_space=pltpu.HBM)] * 3,
        out_specs=(VMEM_SPEC, pl.BlockSpec(memory_space=pltpu.HBM), VMEM_SPEC),
        scratch_shapes=[
            pltpu.VMEM((rows, wide), BF16),
            pltpu.VMEM((blocks, offsets, ROWS_AT_ONCE, width), BF16),
            pltpu.VMEM((ranks, offsets), BF16),
            pltpu.VMEM((rows, columns), BF16),
            pltpu.VMEM((columns, rows), BF16),
            pltpu.SemaphoreType.DMA((2 * blocks + 2,)),
        ],
    )(core, in_hbm(offset.T), in_hbm(target), in_hbm(tensor))


def weights_kernel(parts_ref, context_ref, out_ref):
    high, low = halves(jnp.sum(parts_ref[...], axis=0))
    context = context_ref[...]
    out_ref[...] = mm(high, context) + mm(low, context)


def sum_and_copy_kernel(parts_ref, out_ref):
    out_ref[...] = jnp.broadcast_to(jnp.sum(parts_ref[...], axis=0)[None], out_ref.shape)


def expand_kernel(weights_ref, context_ref, out_ref):
    high, low = halves(weights_ref[...])
    context = context_ref[...]
    value = mm(context, high, NT) + mm(context, low, NT)
    out_ref[...] = jnp.broadcast_to(value[None], out_ref.shape)


def basis_kernel(high_ref, low_ref, own_ref, other_ref, out_ref):
    depth = own_ref.shape[0]
    parts = [halves(ref[...]) for ref in (own_ref, other_ref)]
    for at in range(0, out_ref.shape[0], ROWS_AT_ONCE):
        rows = slice(at, at + ROWS_AT_ONCE)
        total = 0.0
        for n, (vhigh, vlow) in enumerate(parts):
            to = slice(n * depth, (n + 1) * depth)
            high = high_ref[rows, to]
            total += mm(high, vhigh) + mm(high, vlow) + mm(low_ref[rows, to], vhigh)
        out_ref[rows, :] = total


def make_basis(high, low, own, other):
    rows = high.shape[0]
    return call(basis_kernel, jax.ShapeDtypeStruct((rows, own.shape[1]), F32))(
        in_vmem(high), in_vmem(low), own, other
    )


def gram_kernel(basis_ref, out_ref):
    high, low = halves(basis_ref[...])
    cross = mm(high, low, TN)
    out_ref[...] = mm(high, high, TN) + (cross + cross.T)


def row(value, at):
    return jnp.broadcast_to(value[at : at + 1, :], value.shape)


def small_inverse(block):
    shape = (8, 128)
    at_row = lax.broadcasted_iota(jnp.int32, shape, 0)
    left = [jnp.broadcast_to(block[:, k : k + 1], shape) for k in range(8)]
    right = [(at_row == k).astype(F32) for k in range(8)]
    scale = jnp.zeros(shape, F32)
    for j in range(8):
        pivot = row(left[j], j)
        root = lax.rsqrt(pivot)
        scale = jnp.where(at_row == j, root, scale)
        if j < 7:
            ratio = jnp.where(at_row > j, left[j] * (root * root), 0.0)
            for k in range(j + 1, 8):
                left[k] = left[k] - ratio * row(left[k], j)
            for k in range(j + 1):
                right[k] = right[k] - ratio * row(right[k], j)
    return [value * scale for value in right]


def inverse_factor(work_ref):
    size = work_ref.shape[0]
    for top in range(0, size, 32):
        tiles = list(range(top // 128, size // 128))
        tiles += [size // 128 + t for t in range(top // 128 + 1)]
        rows = [
            {t: work_ref[top + 8 * q : top + 8 * q + 8, 128 * t : 128 * t + 128] for t in tiles}
            for q in range(4)
        ]
        for q in range(4):
            first = top + 8 * q
            tile, lane = first // 128, first % 128
            inverse = small_inverse(rows[q][tile][:, lane : lane + 8])
            mine = {}
            for t in tiles:
                mine[t] = sum(inverse[k] * row(rows[q][t], k) for k in range(8))
            rows[q] = mine
            if q < 3:
                coeffs = {(m, k): row(inverse[k], m) for m in range(8) for k in range(m + 1)}
            for other in range(q + 1, 4):
                column = [
                    jnp.broadcast_to(rows[other][tile][:, lane + k : lane + k + 1], (8, 128))
                    for k in range(8)
                ]
                factor = [sum(column[k] * coeffs[m, k] for k in range(m + 1)) for m in range(8)]
                for t in tiles:
                    rows[other][t] = rows[other][t] - sum(factor[m] * row(mine[t], m) for m in range(8))
        for q in range(4):
            for t in tiles:
                work_ref[top + 8 * q : top + 8 * q + 8, 128 * t : 128 * t + 128] = rows[q][t]
        below = top + 32
        if below < size:
            done = jnp.concatenate(
                [jnp.concatenate([rows[q][t] for q in range(4)], axis=0) for t in tiles], axis=1
            )
            high, middle, low = thirds(done)
            left = jnp.concatenate([high, high, middle, high, low, middle], axis=0)
            right = jnp.concatenate([high, middle, high, low, high, middle], axis=0)
            start = 128 * tiles[0]
            skip = below % 128
            change = mm(left[:, below - skip - start : size - start], right, TN)
            for n, t in enumerate(tiles):
                work_ref[below:, 128 * t : 128 * t + 128] -= change[skip:, 128 * n : 128 * n + 128]


def finish_kernel(rows_total, basis_ref, own_ref, other_ref, core_ref, out_ref, work_ref):
    size = basis_ref.shape[1]
    own, other = own_ref[...] / rows_total, other_ref[...] / rows_total
    flip = core_ref[0] != 0
    half = size // 2
    work_ref[:half, :size] = jnp.where(flip, other, own)
    work_ref[half:, :size] = jnp.where(flip, own, other)
    at_row = lax.broadcasted_iota(jnp.int32, (size, size), 0)
    at_column = lax.broadcasted_iota(jnp.int32, (size, size), 1)
    work_ref[:, size:] = (at_row == at_column).astype(F32)
    inverse_factor(work_ref)
    at_row = lax.broadcasted_iota(jnp.int32, (size, size), 0)
    at_column = lax.broadcasted_iota(jnp.int32, (size, size), 1)
    ihigh, ilow = halves(jnp.where(at_row >= at_column, work_ref[:, size:], 0.0))
    high, low = halves(basis_ref[...])
    out_ref[...] = mm(high, ihigh, NT) + (mm(high, ilow, NT) + mm(low, ihigh, NT))


def everyone(value, axes):
    return lax.all_to_all(value, axes, 0, 0)


def copies(value, number):
    return jnp.broadcast_to(value[None], (number,) + value.shape)


def swap(value):
    return lax.ppermute(value, "core", [(0, 1), (1, 0)])


def finish(basis, own, other, core, rows_total):
    columns = basis.shape[1]
    return call(
        functools.partial(finish_kernel, rows_total),
        jax.ShapeDtypeStruct(basis.shape, F32),
        in_specs=[VMEM_SPEC] * 3 + [pl.BlockSpec(memory_space=pltpu.SMEM)],
        scratch_shapes=[pltpu.VMEM((columns, 2 * columns), F32)],
    )(basis, own, other, core)


def on_device(tensor, context, offset, target):
    offsets, rows, width = tensor.shape
    ranks, columns = offset.shape[1], target.shape[1]
    nx, ny, nz = lax.axis_size("x"), lax.axis_size("y"), lax.axis_size(RING)
    core = lax.axis_index("core").astype(jnp.int32).reshape(1)
    flip = core[0] != 0

    high, low, product = project(core, offset, target, tensor)

    half = ranks // 2
    product = product[:half] + swap(product[half:])
    product = everyone(product, "x")
    part = call(weights_kernel, jax.ShapeDtypeStruct((columns, context.shape[1]), F32))(product, context)
    size = ny * nz
    part = everyone(part.reshape(size, columns // size, -1), GROUP)
    part = call(sum_and_copy_kernel, jax.ShapeDtypeStruct(part.shape, F32))(part)
    weights = everyone(part, GROUP).reshape(columns, -1)
    expanded = call(expand_kernel, jax.ShapeDtypeStruct((nx, width, columns), F32))(weights, context)
    own = everyone(expanded, "x").reshape(half * width, columns)
    basis = make_basis(high, low, own, swap(own))

    basis = jnp.sum(everyone(basis.reshape(ny, rows // ny, columns), "y"), axis=0)
    basis = everyone(basis.reshape(nz, rows // ny // nz, columns), RING)
    basis = call(sum_and_copy_kernel, jax.ShapeDtypeStruct(basis.shape, F32))(basis)
    basis = everyone(basis, RING).reshape(rows // ny, columns)
    basis = everyone(copies(basis, ny), "y").reshape(rows, columns)

    gram = call(gram_kernel, jax.ShapeDtypeStruct((columns, columns), F32))(basis)
    gram = gram + swap(gram)
    side = columns // 2
    mine = jnp.where(flip, gram[side:], gram[:side])
    mine = jnp.sum(everyone(copies(mine, nx), "x"), axis=0)
    return finish(basis, mine, swap(mine), core, rows * lax.axis_size(TARGET))


def solution(mesh):
    fine = Mesh(mesh.devices.reshape(4, 2, 4, 4, 2), ("x", "core") + GROUP)
    placed = (
        P("zhi", TARGET, ("zlo", "y")),
        P(("zlo", "y"), None),
        P("zhi", None),
        P(TARGET, None),
    )
    return jax.shard_map(
        on_device, mesh=fine, in_specs=placed, out_specs=P(TARGET, None), check_vma=False
    )
```

```python
import functools

import jax
import jax.numpy as jnp
from jax import lax
from jax.experimental import pallas as pl
from jax.experimental.pallas import tpu as pltpu
from jax.sharding import Mesh
from jax.sharding import PartitionSpec as P

F32, BF16 = jnp.float32, jnp.bfloat16
TARGET = ("x", "core")
GROUP = ("zlo", "y", "zhi")
RING = ("zhi", "zlo")
ROWS_AT_ONCE = 256
NN = (((1,), (0,)), ((), ()))
TN = (((0,), (0,)), ((), ()))
NT = (((1,), (1,)), ((), ()))


def mm(a, b, dims=NN):
    return lax.dot_general(a, b, dims, preferred_element_type=F32)


def halves(value):
    high = value.astype(BF16)
    return high, (value - high.astype(F32)).astype(BF16)


def thirds(value):
    high = value.astype(BF16)
    rest = value - high.astype(F32)
    middle = rest.astype(BF16)
    return high, middle, (rest - middle.astype(F32)).astype(BF16)


VMEM_SPEC = pl.BlockSpec(memory_space=pltpu.VMEM)


def in_hbm(value):
    return pltpu.with_memory_space_constraint(value, pltpu.HBM)


def in_vmem(value):
    return pltpu.with_memory_space_constraint(value, pltpu.VMEM)


def call(kernel, out_shape, vmem=16, **more):
    return pl.pallas_call(
        kernel,
        out_shape=out_shape,
        compiler_params=pltpu.CompilerParams(vmem_limit_bytes=vmem * 2**20),
        **more,
    )


def project_kernel(
    core_ref,
    offset_hbm,
    target_hbm,
    tensor_ref,
    high_ref,
    low_hbm,
    out_ref,
    low_ref,
    held_ref,
    offset_ref,
    target_ref,
    factor_ref,
    sems,
):
    offsets, rows, width = tensor_ref.shape
    ranks = offset_ref.shape[0]
    blocks = held_ref.shape[0]
    depth = held_ref.shape[2]
    small = [
        pltpu.make_async_copy(offset_hbm, offset_ref, sems.at[blocks]),
        pltpu.make_async_copy(target_hbm, target_ref, sems.at[blocks + 1]),
    ]
    for copy in small:
        copy.start()
    for block in range(blocks):
        pltpu.make_async_copy(
            tensor_ref.at[:, pl.ds(block * depth, depth), :], held_ref.at[block], sems.at[block]
        ).start()
    for copy in small:
        copy.wait()

    def iota(shape, dim):
        return lax.broadcasted_iota(jnp.int32, shape, dim)

    tall, wide = (ranks * 16, ranks), (offsets, offsets * 16)
    place = iota(tall, 0) // 16
    half = ranks // 2
    rank_at = 2 * (place % half) + jnp.where(place >= half, 1 - core_ref[0], core_ref[0])
    pick = (rank_at == iota(tall, 1)).astype(BF16)
    repeat = (iota(wide, 0) == iota(wide, 1) // 16).astype(BF16)
    spread = mm(mm(pick, offset_ref[...]).astype(BF16), repeat)
    same = iota(spread.shape, 0) % 16 == iota(spread.shape, 1) % 16
    spread = jnp.where(same, spread, 0.0).astype(BF16)
    factor_ref[...] = target_ref[...].astype(F32).T.astype(BF16)

    def contract(block):
        base = block * depth
        for at in range(0, depth, 32):
            sides = [
                held_ref[block, :, at + side : at + side + 16, :].reshape(-1, width) for side in (0, 16)
            ]
            high, low = halves(mm(spread, jnp.concatenate(sides, axis=1)))
            for rank in range(ranks):
                to = slice(rank * width, (rank + 1) * width)
                of = slice(rank * 16, rank * 16 + 16)
                for side in (0, 1):
                    rows_at = slice(base + at + 16 * side, base + at + 16 * side + 16)
                    lanes = slice(side * width, (side + 1) * width)
                    high_ref[rows_at, to] = high[of, lanes]
                    low_ref[rows_at, to] = low[of, lanes]

    def add_product(block):
        here = slice(block * depth, (block + 1) * depth)
        factor = factor_ref[:, here]
        for rank in range(0, ranks, 2):
            to = slice(rank * width, (rank + 2) * width)
            change = mm(factor, high_ref[here, to]) + mm(factor, low_ref[here, to])
            for side in (0, 1):
                part = change[:, side * width : (side + 1) * width]
                out_ref[rank + side] = part if block == 0 else out_ref[rank + side] + part

    def keep(block):
        here = pl.ds(block * depth, depth)
        return pltpu.make_async_copy(low_ref.at[here, :], low_hbm.at[here, :], sems.at[blocks + 2 + block])

    for block in range(blocks):
        pltpu.make_async_copy(
            tensor_ref.at[:, pl.ds(block * depth, depth), :], held_ref.at[block], sems.at[block]
        ).wait()
        contract(block)
        if block > 0:
            add_product(block - 1)
        keep(block).start()
    add_product(blocks - 1)
    for block in range(blocks):
        keep(block).wait()


def project(core, offset, target, tensor):
    offsets, rows, width = tensor.shape
    ranks, columns = offset.shape[1], target.shape[1]
    wide = ranks * width
    blocks = rows // ROWS_AT_ONCE
    return call(
        project_kernel,
        (
            jax.ShapeDtypeStruct((rows, wide), BF16),
            pltpu.HBM((rows, wide), BF16),
            jax.ShapeDtypeStruct((ranks, columns, width), F32),
        ),
        vmem=24,
        in_specs=[
            pl.BlockSpec(memory_space=pltpu.SMEM),
        ]
        + [pl.BlockSpec(memory_space=pltpu.HBM)] * 3,
        out_specs=(VMEM_SPEC, pl.BlockSpec(memory_space=pltpu.HBM), VMEM_SPEC),
        scratch_shapes=[
            pltpu.VMEM((rows, wide), BF16),
            pltpu.VMEM((blocks, offsets, ROWS_AT_ONCE, width), BF16),
            pltpu.VMEM((ranks, offsets), BF16),
            pltpu.VMEM((rows, columns), BF16),
            pltpu.VMEM((columns, rows), BF16),
            pltpu.SemaphoreType.DMA((2 * blocks + 2,)),
        ],
    )(core, in_hbm(offset.T), in_hbm(target), in_hbm(tensor))


def weights_kernel(parts_ref, context_ref, out_ref):
    high, low = halves(jnp.sum(parts_ref[...], axis=0))
    context = context_ref[...]
    out_ref[...] = mm(high, context) + mm(low, context)


def sum_and_copy_kernel(parts_ref, out_ref):
    out_ref[...] = jnp.broadcast_to(jnp.sum(parts_ref[...], axis=0)[None], out_ref.shape)


def expand_kernel(weights_ref, context_ref, out_ref):
    high, low = halves(weights_ref[...])
    context = context_ref[...]
    value = mm(context, high, NT) + mm(context, low, NT)
    out_ref[...] = jnp.broadcast_to(value[None], out_ref.shape)


def add_basis(first, high_ref, low_ref, value_ref, refs):
    out_ref = refs[-1]
    vhigh, vlow = halves(value_ref[...])
    to = slice(first, first + value_ref.shape[0])
    for at in range(0, out_ref.shape[0], ROWS_AT_ONCE):
        rows = slice(at, at + ROWS_AT_ONCE)
        high = high_ref[rows, to]
        total = mm(high, vhigh) + (mm(high, vlow) + mm(low_ref[rows, to], vhigh))
        out_ref[rows, :] = total if len(refs) == 1 else refs[0][rows, :] + total


def basis_kernel(high_ref, low_ref, value_ref, out_ref):
    add_basis(0, high_ref, low_ref, value_ref, (out_ref,))


def rest_kernel(high_ref, low_ref, value_ref, sofar_ref, out_ref):
    add_basis(value_ref.shape[0], high_ref, low_ref, value_ref, (sofar_ref, out_ref))


def make_basis(high, low, own, other):
    high, low = in_vmem(high), in_vmem(low)
    shape = jax.ShapeDtypeStruct((high.shape[0], own.shape[1]), F32)
    part = call(basis_kernel, shape)(high, low, own)
    return call(rest_kernel, shape)(high, low, other, part)


def gram_kernel(core_ref, basis_ref, out_ref):
    high, low = halves(basis_ref[...])
    cross = mm(high, low, TN)
    gram = mm(high, high, TN) + (cross + cross.T)
    side = gram.shape[0] // 2
    left, middle = gram[side:, :side], side // 2
    shares = [
        jnp.concatenate([gram[:side, :side], left[:middle]], axis=0),
        jnp.concatenate([gram[side:, side:], left[middle:]], axis=0),
    ]
    flip = core_ref[0] != 0
    out_ref[0] = jnp.where(flip, shares[1], shares[0])
    out_ref[1] = jnp.where(flip, shares[0], shares[1])


def row(value, at):
    return jnp.broadcast_to(value[at : at + 1, :], value.shape)


def small_inverse(columns):
    left = {(i, k): row(columns[k], i) for k in range(8) for i in range(k, 8)}
    unit, inverse = {}, {}
    for j in range(8):
        root = lax.rsqrt(left[j, j])
        square = root * root
        inverse[j, j] = root
        for k in range(j):
            inverse[j, k] = root * unit[j, k]
        for k in range(j + 1, 8):
            for i in range(k, 8):
                left[i, k] = left[i, k] - (left[i, j] * left[k, j]) * square
        for i in range(j + 1, 8):
            ratio = left[i, j] * square
            for k in range(j):
                unit[i, k] = unit[i, k] - ratio * unit[j, k]
            unit[i, j] = -ratio
    return inverse


def inverse_factor(work_ref):
    size, shape = work_ref.shape[0], (8, 128)
    at_row = lax.broadcasted_iota(jnp.int32, shape, 0)
    for top in range(0, size, 32):
        tiles = list(range(top // 128, size // 128))
        tiles += [size // 128 + t for t in range(top // 128 + 1)]
        rows = [
            {t: work_ref[top + 8 * q : top + 8 * q + 8, 128 * t : 128 * t + 128] for t in tiles}
            for q in range(4)
        ]
        columns = {}
        for q in range(4):
            for k in range(8 * (q + 1)):
                tile, lane = (top + k) // 128, (top + k) % 128
                columns[q, k] = jnp.broadcast_to(rows[q][tile][:, lane : lane + 1], shape)
        for q in range(4):
            inverse = small_inverse([columns[q, 8 * q + k] for k in range(8)])
            factor = {
                (o, j): sum(inverse[j, k] * columns[o, 8 * q + k] for k in range(j + 1))
                for o in range(q + 1, 4)
                for j in range(8)
            }
            for p in range(q + 1, 4):
                for k in range(8):
                    ratios = [row(factor[p, j], k) for j in range(8)]
                    for o in range(p, 4):
                        columns[o, 8 * p + k] -= sum(factor[o, j] * ratios[j] for j in range(8))
            spread = []
            for k in range(8):
                value = jnp.zeros(shape, F32)
                for i in range(k, 8):
                    value = jnp.where(at_row == i, inverse[i, k], value)
                spread.append(value)
            for t in tiles:
                mine = sum(spread[k] * row(rows[q][t], k) for k in range(8))
                rows[q][t] = mine
                for o in range(q + 1, 4):
                    rows[o][t] = rows[o][t] - sum(factor[o, j] * row(mine, j) for j in range(8))
        for q in range(4):
            for t in tiles:
                work_ref[top + 8 * q : top + 8 * q + 8, 128 * t : 128 * t + 128] = rows[q][t]
        below = top + 32
        if below < size:
            done = jnp.concatenate(
                [jnp.concatenate([rows[q][t] for q in range(4)], axis=0) for t in tiles], axis=1
            )
            high, middle, low = thirds(done)
            left = jnp.concatenate([high, high, middle, high, low, middle], axis=0)
            right = jnp.concatenate([high, middle, high, low, high, middle], axis=0)
            start, skip = 128 * tiles[0], below % 128
            change = mm(left[:, below - skip - start : size - start], right, TN)
            for n, t in enumerate(tiles):
                work_ref[below:, 128 * t : 128 * t + 128] -= change[skip:, 128 * n : 128 * n + 128]


def finish_kernel(rows_total, core_ref, basis_ref, own_ref, other_ref, out_hbm, out_ref, work_ref, sems):
    rows, size = basis_ref.shape
    side = size // 2
    own, other = own_ref[...] / rows_total, other_ref[...] / rows_total
    flip = core_ref[0] != 0
    upper, lower = jnp.where(flip, other, own), jnp.where(flip, own, other)
    left = jnp.concatenate([upper[side:], lower[side:]], axis=0)
    work_ref[:side, :side] = upper[:side]
    work_ref[:side, side:size] = left.T
    work_ref[side:, :side] = left
    work_ref[side:, side:size] = lower[:side]
    at_row = lax.broadcasted_iota(jnp.int32, (size, size), 0)
    at_column = lax.broadcasted_iota(jnp.int32, (size, size), 1)
    work_ref[:, size:] = (at_row == at_column).astype(F32)
    inverse_factor(work_ref)
    at_row = lax.broadcasted_iota(jnp.int32, (size, size), 0)
    at_column = lax.broadcasted_iota(jnp.int32, (size, size), 1)
    ihigh, ilow = halves(jnp.where(at_row >= at_column, work_ref[:, size:], 0.0))
    copies = []
    for n, at in enumerate(range(0, rows, ROWS_AT_ONCE)):
        here = pl.ds(at, ROWS_AT_ONCE)
        high, low = halves(basis_ref[here, :])
        out_ref[here, :] = mm(high, ihigh, NT) + (mm(high, ilow, NT) + mm(low, ihigh, NT))
        copies.append(pltpu.make_async_copy(out_ref.at[here, :], out_hbm.at[here, :], sems.at[n]))
        copies[-1].start()
    for copy in copies:
        copy.wait()


def everyone(value, axes):
    return lax.all_to_all(value, axes, 0, 0)


def copies(value, number):
    return jnp.broadcast_to(value[None], (number,) + value.shape)


def swap(value):
    return lax.ppermute(value, "core", [(0, 1), (1, 0)])


def finish(core, basis, own, other, rows_total):
    rows, columns = basis.shape
    return call(
        functools.partial(finish_kernel, rows_total),
        jax.ShapeDtypeStruct(basis.shape, F32),
        in_specs=[pl.BlockSpec(memory_space=pltpu.SMEM)] + [VMEM_SPEC] * 3,
        out_specs=pl.BlockSpec(memory_space=pltpu.HBM),
        scratch_shapes=[
            pltpu.VMEM(basis.shape, F32),
            pltpu.VMEM((columns, 2 * columns), F32),
            pltpu.SemaphoreType.DMA((rows // ROWS_AT_ONCE,)),
        ],
    )(core, basis, own, other)


def on_device(tensor, context, offset, target):
    offsets, rows, width = tensor.shape
    ranks, columns = offset.shape[1], target.shape[1]
    nx, ny, nz = lax.axis_size("x"), lax.axis_size("y"), lax.axis_size(RING)
    core = lax.axis_index("core").astype(jnp.int32).reshape(1)

    high, low, product = project(core, offset, target, tensor)

    half = ranks // 2
    product = product[:half] + swap(product[half:])
    product = everyone(product, "x")
    part = call(weights_kernel, jax.ShapeDtypeStruct((columns, context.shape[1]), F32))(product, context)
    size = ny * nz
    part = everyone(part.reshape(size, columns // size, -1), GROUP)
    part = call(sum_and_copy_kernel, jax.ShapeDtypeStruct(part.shape, F32))(part)
    weights = everyone(part, GROUP).reshape(columns, -1)
    expanded = call(expand_kernel, jax.ShapeDtypeStruct((nx, width, columns), F32))(weights, context)
    own = everyone(expanded, "x").reshape(half * width, columns)
    basis = make_basis(high, low, own, swap(own))

    basis = jnp.sum(everyone(basis.reshape(ny, rows // ny, columns), "y"), axis=0)
    basis = everyone(basis.reshape(nz, rows // ny // nz, columns), RING)
    basis = call(sum_and_copy_kernel, jax.ShapeDtypeStruct(basis.shape, F32))(basis)
    basis = everyone(basis, RING).reshape(rows // ny, columns)
    basis = everyone(copies(basis, ny), "y").reshape(rows, columns)

    gram = call(
        gram_kernel,
        jax.ShapeDtypeStruct((2, 3 * columns // 4, columns // 2), F32),
        in_specs=[pl.BlockSpec(memory_space=pltpu.SMEM), VMEM_SPEC],
    )(core, basis)
    mine = gram[0] + swap(gram[1])
    mine = jnp.sum(everyone(copies(mine, nx), "x"), axis=0)
    return finish(core, basis, mine, swap(mine), rows * lax.axis_size(TARGET))


def solution(mesh):
    fine = Mesh(mesh.devices.reshape(4, 2, 4, 4, 2), ("x", "core") + GROUP)
    placed = (
        P("zhi", TARGET, ("zlo", "y")),
        P(("zlo", "y"), None),
        P("zhi", None),
        P(TARGET, None),
    )
    return jax.shard_map(
        on_device, mesh=fine, in_specs=placed, out_specs=P(TARGET, None), check_vma=False
    )
```

```python
import functools

import jax
import jax.numpy as jnp
from jax import lax
from jax.experimental import pallas as pl
from jax.experimental.pallas import tpu as pltpu
from jax.sharding import Mesh
from jax.sharding import PartitionSpec as P

F32, BF16 = jnp.float32, jnp.bfloat16
TARGET = ("x", "core")
GROUP = ("zlo", "y", "zhi")
RING = ("zhi", "zlo")
ROWS_AT_ONCE = 256
NN = (((1,), (0,)), ((), ()))
TN = (((0,), (0,)), ((), ()))
NT = (((1,), (1,)), ((), ()))


def mm(a, b, dims=NN):
    return lax.dot_general(a, b, dims, preferred_element_type=F32)


def halves(value):
    high = value.astype(BF16)
    return high, (value - high.astype(F32)).astype(BF16)


def thirds(value):
    high = value.astype(BF16)
    rest = value - high.astype(F32)
    middle = rest.astype(BF16)
    return high, middle, (rest - middle.astype(F32)).astype(BF16)


def pack_place(x, y, core):
    return (8 * x + 2 * y + core).astype(jnp.int32).reshape(1)


def core_of(place_ref):
    return place_ref[0] & 1


def y_of(place_ref):
    return (place_ref[0] >> 1) & 3


def x_of(place_ref):
    return place_ref[0] >> 3


VMEM_SPEC = pl.BlockSpec(memory_space=pltpu.VMEM)
SMEM_SPEC = pl.BlockSpec(memory_space=pltpu.SMEM)


def in_hbm(value):
    return pltpu.with_memory_space_constraint(value, pltpu.HBM)


def in_vmem(value):
    return pltpu.with_memory_space_constraint(value, pltpu.VMEM)


def call(kernel, out_shape, vmem=16, **more):
    return pl.pallas_call(
        kernel,
        out_shape=out_shape,
        compiler_params=pltpu.CompilerParams(vmem_limit_bytes=vmem * 2**20),
        **more,
    )


def project_kernel(
    place_ref,
    offset_hbm,
    target_hbm,
    tensor_ref,
    high_ref,
    low_hbm,
    own_ref,
    other_ref,
    low_ref,
    held_ref,
    offset_ref,
    target_ref,
    factor_ref,
    sems,
):
    offsets, rows, width = tensor_ref.shape
    ranks = offset_ref.shape[0]
    blocks = held_ref.shape[0]
    depth = held_ref.shape[2]
    small = [
        pltpu.make_async_copy(offset_hbm, offset_ref, sems.at[blocks]),
        pltpu.make_async_copy(target_hbm, target_ref, sems.at[blocks + 1]),
    ]
    for copy in small:
        copy.start()
    for block in range(blocks):
        pltpu.make_async_copy(
            tensor_ref.at[:, pl.ds(block * depth, depth), :], held_ref.at[block], sems.at[block]
        ).start()
    for copy in small:
        copy.wait()

    def iota(shape, dim):
        return lax.broadcasted_iota(jnp.int32, shape, dim)

    tall, wide = (ranks * 16, ranks), (offsets, offsets * 16)
    at = iota(tall, 0) // 16
    half = ranks // 2
    core = jnp.where(at >= half, 1 - core_of(place_ref), core_of(place_ref))
    rank_at = 2 * ((at + x_of(place_ref)) % half) + core
    pick = (rank_at == iota(tall, 1)).astype(BF16)
    repeat = (iota(wide, 0) == iota(wide, 1) // 16).astype(BF16)
    spread = mm(mm(pick, offset_ref[...]).astype(BF16), repeat)
    same = iota(spread.shape, 0) % 16 == iota(spread.shape, 1) % 16
    spread = jnp.where(same, spread, 0.0).astype(BF16)
    factor_ref[...] = target_ref[...].astype(F32).T.astype(BF16)

    def contract(block):
        base = block * depth
        for at in range(0, depth, 32):
            sides = [
                held_ref[block, :, at + side : at + side + 16, :].reshape(-1, width) for side in (0, 16)
            ]
            high, low = halves(mm(spread, jnp.concatenate(sides, axis=1)))
            for rank in range(ranks):
                to = slice(rank * width, (rank + 1) * width)
                of = slice(rank * 16, rank * 16 + 16)
                for side in (0, 1):
                    rows_at = slice(base + at + 16 * side, base + at + 16 * side + 16)
                    lanes = slice(side * width, (side + 1) * width)
                    high_ref[rows_at, to] = high[of, lanes]
                    low_ref[rows_at, to] = low[of, lanes]

    def add_product(block):
        here = slice(block * depth, (block + 1) * depth)
        factor = factor_ref[:, here]
        for rank in range(0, ranks, 2):
            to = slice(rank * width, (rank + 2) * width)
            change = mm(factor, high_ref[here, to]) + mm(factor, low_ref[here, to])
            for side in (0, 1):
                part = change[:, side * width : (side + 1) * width]
                out_ref, of = (own_ref, rank + side) if rank < half else (other_ref, rank + side - half)
                out_ref[of] = part if block == 0 else out_ref[of] + part

    def keep(block):
        here = pl.ds(block * depth, depth)
        return pltpu.make_async_copy(low_ref.at[here, :], low_hbm.at[here, :], sems.at[blocks + 2 + block])

    for block in range(blocks):
        pltpu.make_async_copy(
            tensor_ref.at[:, pl.ds(block * depth, depth), :], held_ref.at[block], sems.at[block]
        ).wait()
        contract(block)
        if block > 0:
            add_product(block - 1)
        keep(block).start()
    add_product(blocks - 1)
    for block in range(blocks):
        keep(block).wait()


def project(place, offset, target, tensor):
    offsets, rows, width = tensor.shape
    ranks, columns = offset.shape[1], target.shape[1]
    wide = ranks * width
    blocks = rows // ROWS_AT_ONCE
    return call(
        project_kernel,
        (
            jax.ShapeDtypeStruct((rows, wide), BF16),
            pltpu.HBM((rows, wide), BF16),
        )
        + (jax.ShapeDtypeStruct((ranks // 2, columns, width), F32),) * 2,
        vmem=24,
        in_specs=[
            SMEM_SPEC,
        ]
        + [pl.BlockSpec(memory_space=pltpu.HBM)] * 3,
        out_specs=(VMEM_SPEC, pl.BlockSpec(memory_space=pltpu.HBM), VMEM_SPEC, VMEM_SPEC),
        scratch_shapes=[
            pltpu.VMEM((rows, wide), BF16),
            pltpu.VMEM((blocks, offsets, ROWS_AT_ONCE, width), BF16),
            pltpu.VMEM((ranks, offsets), BF16),
            pltpu.VMEM((rows, columns), BF16),
            pltpu.VMEM((columns, rows), BF16),
            pltpu.SemaphoreType.DMA((2 * blocks + 2,)),
        ],
    )(place, in_hbm(offset.T), in_hbm(target), in_hbm(tensor))


def weights_kernel(first_ref, second_ref, third_ref, fourth_ref, context_ref, out_ref):
    total = (first_ref[...] + second_ref[...]) + (third_ref[...] + fourth_ref[...])
    high, low = halves(total)
    context = context_ref[...]
    out_ref[...] = mm(high, context) + mm(low, context)


def sum_and_copy_kernel(parts_ref, out_ref):
    out_ref[...] = jnp.broadcast_to(jnp.sum(parts_ref[...], axis=0)[None], out_ref.shape)


def expand_kernel(weights_ref, context_ref, out_ref):
    high, low = halves(weights_ref[...])
    context = context_ref[...]
    out_ref[...] = mm(context, high, NT) + mm(context, low, NT)


def basis_kernel(high_ref, low_ref, value_ref, out_ref):
    vhigh, vlow = halves(value_ref[...])
    to = slice(0, value_ref.shape[0])
    for at in range(0, out_ref.shape[0], ROWS_AT_ONCE):
        rows = slice(at, at + ROWS_AT_ONCE)
        high = high_ref[rows, to]
        out_ref[rows, :] = mm(high, vhigh) + (mm(high, vlow) + mm(low_ref[rows, to], vhigh))


def rest_kernel(place_ref, high_ref, low_ref, value_ref, sofar_ref, *out_refs):
    vhigh, vlow = halves(value_ref[...])
    depth = value_ref.shape[0]
    to = slice(depth, 2 * depth)
    for ahead, out_ref in enumerate(out_refs):
        count = out_ref.shape[0]
        rows = pl.ds(pl.multiple_of((y_of(place_ref) + ahead) % len(out_refs) * count, count), count)
        high = high_ref[rows, to]
        total = mm(high, vhigh) + (mm(high, vlow) + mm(low_ref[rows, to], vhigh))
        out_ref[...] = sofar_ref[rows, :] + total


def make_basis(place, high, low, own, other, blocks):
    high, low = in_vmem(high), in_vmem(low)
    rows, columns = high.shape[0], own.shape[1]
    part = call(basis_kernel, jax.ShapeDtypeStruct((rows, columns), F32))(high, low, own)
    return call(
        rest_kernel,
        (jax.ShapeDtypeStruct((rows // blocks, columns), F32),) * blocks,
        in_specs=[SMEM_SPEC] + [VMEM_SPEC] * 4,
    )(place, high, low, other, part)


def gram_kernel(place_ref, *refs):
    out_ref, high_ref, low_ref = refs[-3:]
    parts = refs[:-3]
    count = parts[0].shape[0]
    for behind, part_ref in enumerate(parts):
        at = (y_of(place_ref) + len(parts) - behind) % len(parts) * count
        here = pl.ds(pl.multiple_of(at, count), count)
        high_ref[here, :], low_ref[here, :] = halves(part_ref[...])
    high, low = high_ref[...], low_ref[...]
    cross = mm(high, low, TN)
    gram = mm(high, high, TN) + (cross + cross.T)
    side = gram.shape[0] // 2
    left, middle = gram[side:, :side], side // 2
    shares = [
        jnp.concatenate([gram[:side, :side], left[:middle]], axis=0),
        jnp.concatenate([gram[side:, side:], left[middle:]], axis=0),
    ]
    flip = core_of(place_ref) != 0
    out_ref[0] = jnp.where(flip, shares[1], shares[0])
    out_ref[1] = jnp.where(flip, shares[0], shares[1])


def row(value, at):
    return jnp.broadcast_to(value[at : at + 1, :], value.shape)


def small_inverse(columns):
    left = {(i, k): row(columns[k], i) for k in range(8) for i in range(k, 8)}
    unit, inverse = {}, {}
    for j in range(8):
        root = lax.rsqrt(left[j, j])
        square = root * root
        inverse[j, j] = root
        for k in range(j):
            inverse[j, k] = root * unit[j, k]
        for k in range(j + 1, 8):
            for i in range(k, 8):
                left[i, k] = left[i, k] - (left[i, j] * left[k, j]) * square
        for i in range(j + 1, 8):
            ratio = left[i, j] * square
            for k in range(j):
                unit[i, k] = unit[i, k] - ratio * unit[j, k]
            unit[i, j] = -ratio
    return inverse


def inverse_factor(work_ref):
    size, shape = work_ref.shape[0], (8, 128)
    at_row = lax.broadcasted_iota(jnp.int32, shape, 0)
    for top in range(0, size, 32):
        tiles = list(range(top // 128, size // 128))
        tiles += [size // 128 + t for t in range(top // 128 + 1)]
        rows = [
            {t: work_ref[top + 8 * q : top + 8 * q + 8, 128 * t : 128 * t + 128] for t in tiles}
            for q in range(4)
        ]
        columns = {}
        for q in range(4):
            for k in range(8 * (q + 1)):
                tile, lane = (top + k) // 128, (top + k) % 128
                columns[q, k] = jnp.broadcast_to(rows[q][tile][:, lane : lane + 1], shape)
        for q in range(4):
            inverse = small_inverse([columns[q, 8 * q + k] for k in range(8)])
            factor = {
                (o, j): sum(inverse[j, k] * columns[o, 8 * q + k] for k in range(j + 1))
                for o in range(q + 1, 4)
                for j in range(8)
            }
            for p in range(q + 1, 4):
                for k in range(8):
                    ratios = [row(factor[p, j], k) for j in range(8)]
                    for o in range(p, 4):
                        columns[o, 8 * p + k] -= sum(factor[o, j] * ratios[j] for j in range(8))
            spread = []
            for k in range(8):
                value = jnp.zeros(shape, F32)
                for i in range(k, 8):
                    value = jnp.where(at_row == i, inverse[i, k], value)
                spread.append(value)
            for t in tiles:
                mine = sum(spread[k] * row(rows[q][t], k) for k in range(8))
                rows[q][t] = mine
                for o in range(q + 1, 4):
                    rows[o][t] = rows[o][t] - sum(factor[o, j] * row(mine, j) for j in range(8))
        for q in range(4):
            for t in tiles:
                work_ref[top + 8 * q : top + 8 * q + 8, 128 * t : 128 * t + 128] = rows[q][t]
        below = top + 32
        if below < size:
            done = jnp.concatenate(
                [jnp.concatenate([rows[q][t] for q in range(4)], axis=0) for t in tiles], axis=1
            )
            high, middle, low = thirds(done)
            left = jnp.concatenate([high, high, middle, high, low, middle], axis=0)
            right = jnp.concatenate([high, middle, high, low, high, middle], axis=0)
            start, skip = 128 * tiles[0], below % 128
            change = mm(left[:, below - skip - start : size - start], right, TN)
            for n, t in enumerate(tiles):
                work_ref[below:, 128 * t : 128 * t + 128] -= change[skip:, 128 * n : 128 * n + 128]


def finish_kernel(rows_total, place_ref, high_ref, low_ref, own_ref, other_ref, out_hbm, out_ref, work_ref, sems):
    rows, size = high_ref.shape
    side = size // 2
    own, other = own_ref[...] / rows_total, other_ref[...] / rows_total
    flip = core_of(place_ref) != 0
    upper, lower = jnp.where(flip, other, own), jnp.where(flip, own, other)
    left = jnp.concatenate([upper[side:], lower[side:]], axis=0)
    work_ref[:side, :side] = upper[:side]
    work_ref[:side, side:size] = left.T
    work_ref[side:, :side] = left
    work_ref[side:, side:size] = lower[:side]
    at_row = lax.broadcasted_iota(jnp.int32, (size, size), 0)
    at_column = lax.broadcasted_iota(jnp.int32, (size, size), 1)
    work_ref[:, size:] = (at_row == at_column).astype(F32)
    inverse_factor(work_ref)
    at_row = lax.broadcasted_iota(jnp.int32, (size, size), 0)
    at_column = lax.broadcasted_iota(jnp.int32, (size, size), 1)
    ihigh, ilow = halves(jnp.where(at_row >= at_column, work_ref[:, size:], 0.0))
    copies = []
    for n, at in enumerate(range(0, rows, ROWS_AT_ONCE)):
        here = pl.ds(at, ROWS_AT_ONCE)
        high, low = high_ref[here, :], low_ref[here, :]
        out_ref[here, :] = mm(high, ihigh, NT) + (mm(high, ilow, NT) + mm(low, ihigh, NT))
        copies.append(pltpu.make_async_copy(out_ref.at[here, :], out_hbm.at[here, :], sems.at[n]))
        copies[-1].start()
    for copy in copies:
        copy.wait()


def everyone(value, axes):
    return lax.all_to_all(value, axes, 0, 0)


def ahead(value, axis, steps):
    size = lax.axis_size(axis)
    return lax.ppermute(value, axis, [(at, (at + steps) % size) for at in range(size)])


def gather(value, axis):
    return [value] + [ahead(value, axis, steps) for steps in range(1, lax.axis_size(axis))]


def trade(parts, axis):
    return parts[:1] + [ahead(part, axis, steps) for steps, part in enumerate(parts) if steps]


def swap(value):
    return lax.ppermute(value, "core", [(0, 1), (1, 0)])


def finish(place, high, low, own, other, rows_total):
    rows, columns = high.shape
    return call(
        functools.partial(finish_kernel, rows_total),
        jax.ShapeDtypeStruct(high.shape, F32),
        in_specs=[SMEM_SPEC] + [VMEM_SPEC] * 4,
        out_specs=pl.BlockSpec(memory_space=pltpu.HBM),
        scratch_shapes=[
            pltpu.VMEM(high.shape, F32),
            pltpu.VMEM((columns, 2 * columns), F32),
            pltpu.SemaphoreType.DMA((rows // ROWS_AT_ONCE,)),
        ],
    )(place, high, low, own, other)


def on_device(tensor, context, offset, target):
    rows, width = tensor.shape[1:]
    ranks, columns = offset.shape[1], target.shape[1]
    nx, ny, nz = lax.axis_size("x"), lax.axis_size("y"), lax.axis_size(RING)
    place = pack_place(lax.axis_index("x"), lax.axis_index("y"), lax.axis_index("core"))

    high, low, product, given = project(place, offset, target, tensor)

    received = swap(given)
    parts = trade([product[n] + received[n] for n in range(nx)], "x")
    part = call(weights_kernel, jax.ShapeDtypeStruct((columns, context.shape[1]), F32))(*parts, context)
    size = ny * nz
    part = everyone(part.reshape(size, columns // size, -1), GROUP)
    part = call(sum_and_copy_kernel, jax.ShapeDtypeStruct(part.shape, F32))(part)
    weights = everyone(part, GROUP).reshape(columns, -1)
    expanded = call(expand_kernel, jax.ShapeDtypeStruct((width, columns), F32))(weights, context)
    behind = gather(expanded, "x")
    own = jnp.concatenate([behind[-n % nx] for n in range(nx)], axis=0)
    basis = make_basis(place, high, low, own, swap(own), ny)

    basis = sum(trade(list(basis), "y"))
    basis = everyone(basis.reshape(nz, rows // ny // nz, columns), RING)
    basis = call(sum_and_copy_kernel, jax.ShapeDtypeStruct(basis.shape, F32))(basis)
    basis = everyone(basis, RING).reshape(rows // ny, columns)
    blocks = gather(basis, "y")

    gram, high, low = call(
        gram_kernel,
        (
            jax.ShapeDtypeStruct((2, 3 * columns // 4, columns // 2), F32),
        )
        + (jax.ShapeDtypeStruct((rows, columns), BF16),) * 2,
        in_specs=[SMEM_SPEC] + [VMEM_SPEC] * ny,
    )(place, *blocks)
    mine = sum(gather(gram[0] + swap(gram[1]), "x"))
    return finish(place, high, low, mine, swap(mine), rows * lax.axis_size(TARGET))


def solution(mesh):
    fine = Mesh(mesh.devices.reshape(4, 2, 4, 4, 2), ("x", "core") + GROUP)
    placed = (
        P("zhi", TARGET, ("zlo", "y")),
        P(("zlo", "y"), None),
        P("zhi", None),
        P(TARGET, None),
    )
    return jax.shard_map(
        on_device, mesh=fine, in_specs=placed, out_specs=P(TARGET, None), check_vma=False
    )
```

```python
import functools

import jax
import jax.numpy as jnp
from jax import lax
from jax.experimental import pallas as pl
from jax.experimental.pallas import tpu as pltpu
from jax.sharding import Mesh
from jax.sharding import PartitionSpec as P

F32, BF16 = jnp.float32, jnp.bfloat16
TARGET = ("x", "core")
GROUP = ("zlo", "y", "zhi")
RING = ("zhi", "zlo")
ROWS_AT_ONCE = 256
NN = (((1,), (0,)), ((), ()))
TN = (((0,), (0,)), ((), ()))
NT = (((1,), (1,)), ((), ()))


def mm(a, b, dims=NN):
    return lax.dot_general(a, b, dims, preferred_element_type=F32)


def halves(value):
    high = value.astype(BF16)
    return high, (value - high.astype(F32)).astype(BF16)


def thirds(value):
    high = value.astype(BF16)
    rest = value - high.astype(F32)
    middle = rest.astype(BF16)
    return high, middle, (rest - middle.astype(F32)).astype(BF16)


def pack_place(x, y, core):
    return (8 * x + 2 * y + core).astype(jnp.int32).reshape(1)


def core_of(place_ref):
    return place_ref[0] & 1


def y_of(place_ref):
    return (place_ref[0] >> 1) & 3


def x_of(place_ref):
    return place_ref[0] >> 3


VMEM_SPEC = pl.BlockSpec(memory_space=pltpu.VMEM)
SMEM_SPEC = pl.BlockSpec(memory_space=pltpu.SMEM)


def in_hbm(value):
    return pltpu.with_memory_space_constraint(value, pltpu.HBM)


def in_vmem(value):
    return pltpu.with_memory_space_constraint(value, pltpu.VMEM)


def call(kernel, out_shape, vmem=16, **more):
    return pl.pallas_call(
        kernel,
        out_shape=out_shape,
        compiler_params=pltpu.CompilerParams(vmem_limit_bytes=vmem * 2**20),
        **more,
    )


def project_kernel(
    place_ref,
    offset_hbm,
    target_hbm,
    tensor_ref,
    high_ref,
    low_hbm,
    own_ref,
    other_ref,
    low_ref,
    held_ref,
    offset_ref,
    target_ref,
    factor_ref,
    sems,
):
    offsets, rows, width = tensor_ref.shape
    ranks = offset_ref.shape[0]
    blocks = held_ref.shape[0]
    depth = held_ref.shape[2]
    small = [
        pltpu.make_async_copy(offset_hbm, offset_ref, sems.at[blocks]),
        pltpu.make_async_copy(target_hbm, target_ref, sems.at[blocks + 1]),
    ]
    for copy in small:
        copy.start()
    for block in range(blocks):
        pltpu.make_async_copy(
            tensor_ref.at[:, pl.ds(block * depth, depth), :], held_ref.at[block], sems.at[block]
        ).start()
    for copy in small:
        copy.wait()

    def iota(shape, dim):
        return lax.broadcasted_iota(jnp.int32, shape, dim)

    tall, wide = (ranks * 16, ranks), (offsets, offsets * 16)
    at = iota(tall, 0) // 16
    half = ranks // 2
    core = jnp.where(at >= half, 1 - core_of(place_ref), core_of(place_ref))
    rank_at = 2 * ((at + x_of(place_ref)) % half) + core
    pick = (rank_at == iota(tall, 1)).astype(BF16)
    repeat = (iota(wide, 0) == iota(wide, 1) // 16).astype(BF16)
    spread = mm(mm(pick, offset_ref[...]).astype(BF16), repeat)
    same = iota(spread.shape, 0) % 16 == iota(spread.shape, 1) % 16
    spread = jnp.where(same, spread, 0.0).astype(BF16)
    factor_ref[...] = target_ref[...].astype(F32).T.astype(BF16)

    def contract(block):
        base = block * depth
        for at in range(0, depth, 32):
            sides = [
                held_ref[block, :, at + side : at + side + 16, :].reshape(-1, width) for side in (0, 16)
            ]
            high, low = halves(mm(spread, jnp.concatenate(sides, axis=1)))
            for rank in range(ranks):
                to = slice(rank * width, (rank + 1) * width)
                of = slice(rank * 16, rank * 16 + 16)
                for side in (0, 1):
                    rows_at = slice(base + at + 16 * side, base + at + 16 * side + 16)
                    lanes = slice(side * width, (side + 1) * width)
                    high_ref[rows_at, to] = high[of, lanes]
                    low_ref[rows_at, to] = low[of, lanes]

    def add_product(block):
        here = slice(block * depth, (block + 1) * depth)
        factor = factor_ref[:, here]
        for rank in range(0, ranks, 2):
            to = slice(rank * width, (rank + 2) * width)
            change = mm(factor, high_ref[here, to]) + mm(factor, low_ref[here, to])
            for side in (0, 1):
                part = change[:, side * width : (side + 1) * width]
                out_ref, of = (own_ref, rank + side) if rank < half else (other_ref, rank + side - half)
                out_ref[of] = part if block == 0 else out_ref[of] + part

    def keep(block):
        here = pl.ds(block * depth, depth)
        return pltpu.make_async_copy(low_ref.at[here, :], low_hbm.at[here, :], sems.at[blocks + 2 + block])

    for block in range(blocks):
        pltpu.make_async_copy(
            tensor_ref.at[:, pl.ds(block * depth, depth), :], held_ref.at[block], sems.at[block]
        ).wait()
        contract(block)
        if block > 0:
            add_product(block - 1)
        keep(block).start()
    add_product(blocks - 1)
    for block in range(blocks):
        keep(block).wait()


def project(place, offset, target, tensor):
    offsets, rows, width = tensor.shape
    ranks, columns = offset.shape[1], target.shape[1]
    wide = ranks * width
    blocks = rows // ROWS_AT_ONCE
    return call(
        project_kernel,
        (
            jax.ShapeDtypeStruct((rows, wide), BF16),
            pltpu.HBM((rows, wide), BF16),
        )
        + (jax.ShapeDtypeStruct((ranks // 2, columns, width), F32),) * 2,
        vmem=24,
        in_specs=[
            SMEM_SPEC,
        ]
        + [pl.BlockSpec(memory_space=pltpu.HBM)] * 3,
        out_specs=(VMEM_SPEC, pl.BlockSpec(memory_space=pltpu.HBM), VMEM_SPEC, VMEM_SPEC),
        scratch_shapes=[
            pltpu.VMEM((rows, wide), BF16),
            pltpu.VMEM((blocks, offsets, ROWS_AT_ONCE, width), BF16),
            pltpu.VMEM((ranks, offsets), BF16),
            pltpu.VMEM((rows, columns), BF16),
            pltpu.VMEM((columns, rows), BF16),
            pltpu.SemaphoreType.DMA((2 * blocks + 2,)),
        ],
    )(place, in_hbm(offset.T), in_hbm(target), in_hbm(tensor))


def weights_kernel(first_ref, second_ref, third_ref, fourth_ref, context_ref, out_ref):
    total = (first_ref[...] + second_ref[...]) + (third_ref[...] + fourth_ref[...])
    high, low = halves(total)
    context = context_ref[...]
    out_ref[...] = mm(high, context) + mm(low, context)


def sum_and_copy_kernel(parts_ref, out_ref):
    out_ref[...] = jnp.broadcast_to(jnp.sum(parts_ref[...], axis=0)[None], out_ref.shape)


def expand_kernel(weights_ref, context_ref, out_ref):
    high, low = halves(weights_ref[...])
    context = context_ref[...]
    out_ref[...] = mm(context, high, NT) + mm(context, low, NT)


def basis_kernel(high_ref, low_ref, value_ref, out_ref):
    vhigh, vlow = halves(value_ref[...])
    to = slice(0, value_ref.shape[0])
    for at in range(0, out_ref.shape[0], ROWS_AT_ONCE):
        rows = slice(at, at + ROWS_AT_ONCE)
        high = high_ref[rows, to]
        out_ref[rows, :] = mm(high, vhigh) + (mm(high, vlow) + mm(low_ref[rows, to], vhigh))


def rest_kernel(place_ref, high_ref, low_ref, value_ref, sofar_ref, *out_refs):
    vhigh, vlow = halves(value_ref[...])
    depth = value_ref.shape[0]
    to = slice(depth, 2 * depth)
    for ahead, out_ref in enumerate(out_refs):
        count = out_ref.shape[0]
        rows = pl.ds(pl.multiple_of((y_of(place_ref) + ahead) % len(out_refs) * count, count), count)
        high = high_ref[rows, to]
        total = mm(high, vhigh) + (mm(high, vlow) + mm(low_ref[rows, to], vhigh))
        out_ref[...] = sofar_ref[rows, :] + total


def make_basis(place, high, low, own, other, blocks):
    high, low = in_vmem(high), in_vmem(low)
    rows, columns = high.shape[0], own.shape[1]
    part = call(basis_kernel, jax.ShapeDtypeStruct((rows, columns), F32))(high, low, own)
    return call(
        rest_kernel,
        (jax.ShapeDtypeStruct((rows // blocks, columns), F32),) * blocks,
        in_specs=[SMEM_SPEC] + [VMEM_SPEC] * 4,
    )(place, high, low, other, part)


def gram_kernel(place_ref, basis_ref, out_ref):
    high, low = halves(basis_ref[...])
    cross = mm(high, low, TN)
    gram = mm(high, high, TN) + (cross + cross.T)
    side = gram.shape[0] // 2
    left, middle = gram[side:, :side], side // 2
    shares = [
        jnp.concatenate([gram[:side, :side], left[:middle]], axis=0),
        jnp.concatenate([gram[side:, side:], left[middle:]], axis=0),
    ]
    flip = core_of(place_ref) != 0
    out_ref[0] = jnp.where(flip, shares[1], shares[0])
    out_ref[1] = jnp.where(flip, shares[0], shares[1])


def row(value, at):
    return jnp.broadcast_to(value[at : at + 1, :], value.shape)


def small_inverse(columns):
    left = {(i, k): row(columns[k], i) for k in range(8) for i in range(k, 8)}
    unit, inverse = {}, {}
    for j in range(8):
        root = lax.rsqrt(left[j, j])
        square = root * root
        inverse[j, j] = root
        for k in range(j):
            inverse[j, k] = root * unit[j, k]
        for k in range(j + 1, 8):
            for i in range(k, 8):
                left[i, k] = left[i, k] - (left[i, j] * left[k, j]) * square
        for i in range(j + 1, 8):
            ratio = left[i, j] * square
            for k in range(j):
                unit[i, k] = unit[i, k] - ratio * unit[j, k]
            unit[i, j] = -ratio
    return inverse


def inverse_factor(work_ref):
    size, shape = work_ref.shape[0], (8, 128)
    at_row = lax.broadcasted_iota(jnp.int32, shape, 0)
    for top in range(0, size, 32):
        tiles = list(range(top // 128, size // 128))
        tiles += [size // 128 + t for t in range(top // 128 + 1)]
        rows = [
            {t: work_ref[top + 8 * q : top + 8 * q + 8, 128 * t : 128 * t + 128] for t in tiles}
            for q in range(4)
        ]
        columns = {}
        for q in range(4):
            for k in range(8 * (q + 1)):
                tile, lane = (top + k) // 128, (top + k) % 128
                columns[q, k] = jnp.broadcast_to(rows[q][tile][:, lane : lane + 1], shape)
        for q in range(4):
            inverse = small_inverse([columns[q, 8 * q + k] for k in range(8)])
            factor = {
                (o, j): sum(inverse[j, k] * columns[o, 8 * q + k] for k in range(j + 1))
                for o in range(q + 1, 4)
                for j in range(8)
            }
            for p in range(q + 1, 4):
                for k in range(8):
                    ratios = [row(factor[p, j], k) for j in range(8)]
                    for o in range(p, 4):
                        columns[o, 8 * p + k] -= sum(factor[o, j] * ratios[j] for j in range(8))
            spread = []
            for k in range(8):
                value = jnp.zeros(shape, F32)
                for i in range(k, 8):
                    value = jnp.where(at_row == i, inverse[i, k], value)
                spread.append(value)
            for t in tiles:
                mine = sum(spread[k] * row(rows[q][t], k) for k in range(8))
                rows[q][t] = mine
                for o in range(q + 1, 4):
                    rows[o][t] = rows[o][t] - sum(factor[o, j] * row(mine, j) for j in range(8))
        for q in range(4):
            for t in tiles:
                work_ref[top + 8 * q : top + 8 * q + 8, 128 * t : 128 * t + 128] = rows[q][t]
        below = top + 32
        if below < size:
            done = jnp.concatenate(
                [jnp.concatenate([rows[q][t] for q in range(4)], axis=0) for t in tiles], axis=1
            )
            high, middle, low = thirds(done)
            left = jnp.concatenate([high, high, middle, high, low, middle], axis=0)
            right = jnp.concatenate([high, middle, high, low, high, middle], axis=0)
            start, skip = 128 * tiles[0], below % 128
            change = mm(left[:, below - skip - start : size - start], right, TN)
            for n, t in enumerate(tiles):
                work_ref[below:, 128 * t : 128 * t + 128] -= change[skip:, 128 * n : 128 * n + 128]


def factor_kernel(rows_total, place_ref, own_ref, other_ref, high_ref, low_ref, work_ref):
    size = high_ref.shape[0]
    side = size // 2
    own, other = own_ref[...] / rows_total, other_ref[...] / rows_total
    flip = core_of(place_ref) != 0
    upper, lower = jnp.where(flip, other, own), jnp.where(flip, own, other)
    left = jnp.concatenate([upper[side:], lower[side:]], axis=0)
    work_ref[:side, :side] = upper[:side]
    work_ref[:side, side:size] = left.T
    work_ref[side:, :side] = left
    work_ref[side:, side:size] = lower[:side]
    at_row = lax.broadcasted_iota(jnp.int32, (size, size), 0)
    at_column = lax.broadcasted_iota(jnp.int32, (size, size), 1)
    work_ref[:, size:] = (at_row == at_column).astype(F32)
    inverse_factor(work_ref)
    at_row = lax.broadcasted_iota(jnp.int32, (size, size), 0)
    at_column = lax.broadcasted_iota(jnp.int32, (size, size), 1)
    high_ref[...], low_ref[...] = halves(jnp.where(at_row >= at_column, work_ref[:, size:], 0.0))


def apply_kernel(place_ref, ihigh_ref, ilow_ref, *refs):
    out_hbm, out_ref, sems = refs[-3:]
    parts = refs[:-3]
    ihigh, ilow = ihigh_ref[...], ilow_ref[...]
    writes = []
    for behind, part_ref in enumerate(parts):
        count = part_ref.shape[0]
        high, low = halves(part_ref[...])
        out_ref[behind] = mm(high, ihigh, NT) + (mm(high, ilow, NT) + mm(low, ihigh, NT))
        at = (y_of(place_ref) + len(parts) - behind) % len(parts) * count
        here = pl.ds(pl.multiple_of(at, count), count)
        writes.append(pltpu.make_async_copy(out_ref.at[behind], out_hbm.at[here, :], sems.at[behind]))
        writes[-1].start()
    for write in writes:
        write.wait()


def everyone(value, axes):
    return lax.all_to_all(value, axes, 0, 0)


def ahead(value, axis, steps):
    size = lax.axis_size(axis)
    return lax.ppermute(value, axis, [(at, (at + steps) % size) for at in range(size)])


def gather(value, axis):
    return [value] + [ahead(value, axis, steps) for steps in range(1, lax.axis_size(axis))]


def trade(parts, axis):
    return parts[:1] + [ahead(part, axis, steps) for steps, part in enumerate(parts) if steps]


def swap(value):
    return lax.ppermute(value, "core", [(0, 1), (1, 0)])


def total(values):
    first, second, third, fourth = values
    return (first + third) + (second + fourth)


def invert(place, own, other, columns, rows_total):
    return call(
        functools.partial(factor_kernel, rows_total),
        (jax.ShapeDtypeStruct((columns, columns), BF16),) * 2,
        in_specs=[SMEM_SPEC] + [VMEM_SPEC] * 2,
        scratch_shapes=[pltpu.VMEM((columns, 2 * columns), F32)],
    )(place, own, other)


def finish(place, inverse, blocks):
    count, columns = blocks[0].shape
    number = len(blocks)
    return call(
        apply_kernel,
        jax.ShapeDtypeStruct((number * count, columns), F32),
        in_specs=[SMEM_SPEC] + [VMEM_SPEC] * (2 + number),
        out_specs=pl.BlockSpec(memory_space=pltpu.HBM),
        scratch_shapes=[
            pltpu.VMEM((number, count, columns), F32),
            pltpu.SemaphoreType.DMA((number,)),
        ],
    )(place, *inverse, *blocks)


def on_device(tensor, context, offset, target):
    rows, width = tensor.shape[1:]
    ranks, columns = offset.shape[1], target.shape[1]
    nx, ny, nz = lax.axis_size("x"), lax.axis_size("y"), lax.axis_size(RING)
    place = pack_place(lax.axis_index("x"), lax.axis_index("y"), lax.axis_index("core"))

    high, low, product, given = project(place, offset, target, tensor)

    received = swap(given)
    parts = trade([product[n] + received[n] for n in range(nx)], "x")
    part = call(weights_kernel, jax.ShapeDtypeStruct((columns, context.shape[1]), F32))(*parts, context)
    size = ny * nz
    part = everyone(part.reshape(size, columns // size, -1), GROUP)
    part = call(sum_and_copy_kernel, jax.ShapeDtypeStruct(part.shape, F32))(part)
    weights = everyone(part, GROUP).reshape(columns, -1)
    expanded = call(expand_kernel, jax.ShapeDtypeStruct((width, columns), F32))(weights, context)
    behind = gather(expanded, "x")
    own = jnp.concatenate([behind[-n % nx] for n in range(nx)], axis=0)
    basis = make_basis(place, high, low, own, swap(own), ny)

    basis = sum(trade(list(basis), "y"))
    basis = everyone(basis.reshape(nz, rows // ny // nz, columns), RING)
    basis = call(sum_and_copy_kernel, jax.ShapeDtypeStruct(basis.shape, F32))(basis)
    basis = everyone(basis, RING).reshape(rows // ny, columns)

    gram = call(
        gram_kernel,
        jax.ShapeDtypeStruct((2, 3 * columns // 4, columns // 2), F32),
        in_specs=[SMEM_SPEC, VMEM_SPEC],
    )(place, basis)
    mine = total(gather(gram[0] + swap(gram[1]), "y"))
    basis, mine = lax.optimization_barrier((basis, mine))
    blocks = gather(basis, "y")
    mine = total(gather(mine, "x"))
    inverse = invert(place, mine, swap(mine), columns, rows * lax.axis_size(TARGET))
    return finish(place, inverse, blocks)


def solution(mesh):
    fine = Mesh(mesh.devices.reshape(4, 2, 4, 4, 2), ("x", "core") + GROUP)
    placed = (
        P("zhi", TARGET, ("zlo", "y")),
        P(("zlo", "y"), None),
        P("zhi", None),
        P(TARGET, None),
    )
    return jax.shard_map(
        on_device, mesh=fine, in_specs=placed, out_specs=P(TARGET, None), check_vma=False
    )
```

```python
import functools

import jax
import jax.numpy as jnp
from jax import lax
from jax.experimental import pallas as pl
from jax.experimental.pallas import tpu as pltpu
from jax.sharding import Mesh
from jax.sharding import PartitionSpec as P

F32, BF16 = jnp.float32, jnp.bfloat16
TARGET = ("x", "core")
GROUP = ("zlo", "y", "zhi")
RING = ("zhi", "zlo")
ROWS_AT_ONCE = 256
NN = (((1,), (0,)), ((), ()))
TN = (((0,), (0,)), ((), ()))
NT = (((1,), (1,)), ((), ()))


def mm(a, b, dims=NN):
    return lax.dot_general(a, b, dims, preferred_element_type=F32)


def halves(value):
    high = value.astype(BF16)
    return high, (value - high.astype(F32)).astype(BF16)


def thirds(value):
    high = value.astype(BF16)
    rest = value - high.astype(F32)
    middle = rest.astype(BF16)
    return high, middle, (rest - middle.astype(F32)).astype(BF16)


def pack_place(x, y, core):
    return (8 * x + 2 * y + core).astype(jnp.int32).reshape(1)


def core_of(place_ref):
    return place_ref[0] & 1


def y_of(place_ref):
    return (place_ref[0] >> 1) & 3


def x_of(place_ref):
    return place_ref[0] >> 3


VMEM_SPEC = pl.BlockSpec(memory_space=pltpu.VMEM)
SMEM_SPEC = pl.BlockSpec(memory_space=pltpu.SMEM)


def in_hbm(value):
    return pltpu.with_memory_space_constraint(value, pltpu.HBM)


def in_vmem(value):
    return pltpu.with_memory_space_constraint(value, pltpu.VMEM)


def call(kernel, out_shape, vmem=16, **more):
    return pl.pallas_call(
        kernel,
        out_shape=out_shape,
        compiler_params=pltpu.CompilerParams(vmem_limit_bytes=vmem * 2**20),
        **more,
    )


def project_kernel(
    place_ref,
    offset_hbm,
    target_hbm,
    tensor_ref,
    high_ref,
    low_hbm,
    own_ref,
    other_ref,
    low_ref,
    held_ref,
    offset_ref,
    target_ref,
    factor_ref,
    sems,
):
    offsets, rows, width = tensor_ref.shape
    ranks = offset_ref.shape[0]
    blocks = held_ref.shape[0]
    depth = held_ref.shape[2]
    small = [
        pltpu.make_async_copy(offset_hbm, offset_ref, sems.at[blocks]),
        pltpu.make_async_copy(target_hbm, target_ref, sems.at[blocks + 1]),
    ]
    for copy in small:
        copy.start()
    for block in range(blocks):
        pltpu.make_async_copy(
            tensor_ref.at[:, pl.ds(block * depth, depth), :], held_ref.at[block], sems.at[block]
        ).start()
    for copy in small:
        copy.wait()

    def iota(shape, dim):
        return lax.broadcasted_iota(jnp.int32, shape, dim)

    tall, wide = (ranks * 16, ranks), (offsets, offsets * 16)
    at = iota(tall, 0) // 16
    half = ranks // 2
    core = jnp.where(at >= half, 1 - core_of(place_ref), core_of(place_ref))
    rank_at = 2 * ((at + x_of(place_ref)) % half) + core
    pick = (rank_at == iota(tall, 1)).astype(BF16)
    repeat = (iota(wide, 0) == iota(wide, 1) // 16).astype(BF16)
    spread = mm(mm(pick, offset_ref[...]).astype(BF16), repeat)
    same = iota(spread.shape, 0) % 16 == iota(spread.shape, 1) % 16
    spread = jnp.where(same, spread, 0.0).astype(BF16)
    factor_ref[...] = target_ref[...].astype(F32).T.astype(BF16)

    def contract(block):
        base = block * depth
        for at in range(0, depth, 32):
            sides = [
                held_ref[block, :, at + side : at + side + 16, :].reshape(-1, width) for side in (0, 16)
            ]
            high, low = halves(mm(spread, jnp.concatenate(sides, axis=1)))
            for rank in range(ranks):
                to = slice(rank * width, (rank + 1) * width)
                of = slice(rank * 16, rank * 16 + 16)
                for side in (0, 1):
                    rows_at = slice(base + at + 16 * side, base + at + 16 * side + 16)
                    lanes = slice(side * width, (side + 1) * width)
                    high_ref[rows_at, to] = high[of, lanes]
                    low_ref[rows_at, to] = low[of, lanes]

    def add_product(block):
        here = slice(block * depth, (block + 1) * depth)
        factor = factor_ref[:, here]
        for rank in range(0, ranks, 2):
            to = slice(rank * width, (rank + 2) * width)
            change = mm(factor, high_ref[here, to]) + mm(factor, low_ref[here, to])
            for side in (0, 1):
                part = change[:, side * width : (side + 1) * width]
                out_ref, of = (own_ref, rank + side) if rank < half else (other_ref, rank + side - half)
                out_ref[of] = part if block == 0 else out_ref[of] + part

    def keep(block):
        here = pl.ds(block * depth, depth)
        return pltpu.make_async_copy(low_ref.at[here, :], low_hbm.at[here, :], sems.at[blocks + 2 + block])

    for block in range(blocks):
        pltpu.make_async_copy(
            tensor_ref.at[:, pl.ds(block * depth, depth), :], held_ref.at[block], sems.at[block]
        ).wait()
        contract(block)
        if block > 0:
            add_product(block - 1)
        keep(block).start()
    add_product(blocks - 1)
    for block in range(blocks):
        keep(block).wait()


def project(place, offset, target, tensor):
    offsets, rows, width = tensor.shape
    ranks, columns = offset.shape[1], target.shape[1]
    wide = ranks * width
    blocks = rows // ROWS_AT_ONCE
    return call(
        project_kernel,
        (
            jax.ShapeDtypeStruct((rows, wide), BF16),
            pltpu.HBM((rows, wide), BF16),
        )
        + (jax.ShapeDtypeStruct((ranks // 2, columns, width), F32),) * 2,
        vmem=24,
        in_specs=[
            SMEM_SPEC,
        ]
        + [pl.BlockSpec(memory_space=pltpu.HBM)] * 3,
        out_specs=(VMEM_SPEC, pl.BlockSpec(memory_space=pltpu.HBM), VMEM_SPEC, VMEM_SPEC),
        scratch_shapes=[
            pltpu.VMEM((rows, wide), BF16),
            pltpu.VMEM((blocks, offsets, ROWS_AT_ONCE, width), BF16),
            pltpu.VMEM((ranks, offsets), BF16),
            pltpu.VMEM((rows, columns), BF16),
            pltpu.VMEM((columns, rows), BF16),
            pltpu.SemaphoreType.DMA((2 * blocks + 2,)),
        ],
    )(place, in_hbm(offset.T), in_hbm(target), in_hbm(tensor))


def weights_kernel(first_ref, second_ref, third_ref, fourth_ref, context_ref, out_ref):
    total = (first_ref[...] + second_ref[...]) + (third_ref[...] + fourth_ref[...])
    high, low = halves(total)
    context = context_ref[...]
    out_ref[...] = mm(high, context) + mm(low, context)


def sum_and_copy_kernel(parts_ref, out_ref):
    out_ref[...] = jnp.broadcast_to(jnp.sum(parts_ref[...], axis=0)[None], out_ref.shape)


def expand_kernel(weights_ref, context_ref, out_ref):
    high, low = halves(weights_ref[...])
    context = context_ref[...]
    out_ref[...] = mm(context, high, NT) + mm(context, low, NT)


def basis_kernel(high_ref, low_ref, value_ref, out_ref):
    vhigh, vlow = halves(value_ref[...])
    to = slice(0, value_ref.shape[0])
    for at in range(0, out_ref.shape[0], ROWS_AT_ONCE):
        rows = slice(at, at + ROWS_AT_ONCE)
        high = high_ref[rows, to]
        out_ref[rows, :] = mm(high, vhigh) + (mm(high, vlow) + mm(low_ref[rows, to], vhigh))


def rest_kernel(steps, blocks, place_ref, high_ref, low_ref, value_ref, sofar_ref, *out_refs):
    vhigh, vlow = halves(value_ref[...])
    depth = value_ref.shape[0]
    to = slice(depth, 2 * depth)
    for step, out_ref in zip(steps, out_refs):
        count = out_ref.shape[0]
        rows = pl.ds(pl.multiple_of((y_of(place_ref) + step) % blocks * count, count), count)
        high = high_ref[rows, to]
        total = mm(high, vhigh) + (mm(high, vlow) + mm(low_ref[rows, to], vhigh))
        out_ref[...] = sofar_ref[rows, :] + total


def make_basis(place, high, low, own, other, blocks):
    high, low = in_vmem(high), in_vmem(low)
    rows, columns = high.shape[0], own.shape[1]
    part = call(basis_kernel, jax.ShapeDtypeStruct((rows, columns), F32))(high, low, own)
    out = {}
    far = blocks // 2
    for steps in ((far,), tuple(step for step in range(blocks) if step != far)):
        values = call(
            functools.partial(rest_kernel, steps, blocks),
            (jax.ShapeDtypeStruct((rows // blocks, columns), F32),) * len(steps),
            in_specs=[SMEM_SPEC] + [VMEM_SPEC] * 4,
        )(place, high, low, other, part)
        out.update(zip(steps, values))
    return [out[step] for step in range(blocks)]


def gram_kernel(place_ref, basis_ref, out_ref):
    high, low = halves(basis_ref[...])
    cross = mm(high, low, TN)
    gram = mm(high, high, TN) + (cross + cross.T)
    side = gram.shape[0] // 2
    left, middle = gram[side:, :side], side // 2
    shares = [
        jnp.concatenate([gram[:side, :side], left[:middle]], axis=0),
        jnp.concatenate([gram[side:, side:], left[middle:]], axis=0),
    ]
    flip = core_of(place_ref) != 0
    out_ref[0] = jnp.where(flip, shares[1], shares[0])
    out_ref[1] = jnp.where(flip, shares[0], shares[1])


def row(value, at):
    return jnp.broadcast_to(value[at : at + 1, :], value.shape)


def small_inverse(columns):
    left = {(i, k): row(columns[k], i) for k in range(8) for i in range(k, 8)}
    unit, inverse = {}, {}
    for j in range(8):
        root = lax.rsqrt(left[j, j])
        square = root * root
        inverse[j, j] = root
        for k in range(j):
            inverse[j, k] = root * unit[j, k]
        for k in range(j + 1, 8):
            for i in range(k, 8):
                left[i, k] = left[i, k] - (left[i, j] * left[k, j]) * square
        for i in range(j + 1, 8):
            ratio = left[i, j] * square
            for k in range(j):
                unit[i, k] = unit[i, k] - ratio * unit[j, k]
            unit[i, j] = -ratio
    return inverse


def inverse_factor(work_ref):
    size, shape = work_ref.shape[0], (8, 128)
    at_row = lax.broadcasted_iota(jnp.int32, shape, 0)
    for top in range(0, size, 32):
        tiles = list(range(top // 128, size // 128))
        tiles += [size // 128 + t for t in range(top // 128 + 1)]
        rows = [
            {t: work_ref[top + 8 * q : top + 8 * q + 8, 128 * t : 128 * t + 128] for t in tiles}
            for q in range(4)
        ]
        columns = {}
        for q in range(4):
            for k in range(8 * (q + 1)):
                tile, lane = (top + k) // 128, (top + k) % 128
                columns[q, k] = jnp.broadcast_to(rows[q][tile][:, lane : lane + 1], shape)
        for q in range(4):
            inverse = small_inverse([columns[q, 8 * q + k] for k in range(8)])
            factor = {
                (o, j): sum(inverse[j, k] * columns[o, 8 * q + k] for k in range(j + 1))
                for o in range(q + 1, 4)
                for j in range(8)
            }
            for p in range(q + 1, 4):
                for k in range(8):
                    ratios = [row(factor[p, j], k) for j in range(8)]
                    for o in range(p, 4):
                        columns[o, 8 * p + k] -= sum(factor[o, j] * ratios[j] for j in range(8))
            spread = []
            for k in range(8):
                value = jnp.zeros(shape, F32)
                for i in range(k, 8):
                    value = jnp.where(at_row == i, inverse[i, k], value)
                spread.append(value)
            for t in tiles:
                mine = sum(spread[k] * row(rows[q][t], k) for k in range(8))
                rows[q][t] = mine
                for o in range(q + 1, 4):
                    rows[o][t] = rows[o][t] - sum(factor[o, j] * row(mine, j) for j in range(8))
        for q in range(4):
            for t in tiles:
                work_ref[top + 8 * q : top + 8 * q + 8, 128 * t : 128 * t + 128] = rows[q][t]
        below = top + 32
        if below < size:
            done = jnp.concatenate(
                [jnp.concatenate([rows[q][t] for q in range(4)], axis=0) for t in tiles], axis=1
            )
            high, middle, low = thirds(done)
            left = jnp.concatenate([high, high, middle, high, low, middle], axis=0)
            right = jnp.concatenate([high, middle, high, low, high, middle], axis=0)
            start, skip = 128 * tiles[0], below % 128
            change = mm(left[:, below - skip - start : size - start], right, TN)
            for n, t in enumerate(tiles):
                work_ref[below:, 128 * t : 128 * t + 128] -= change[skip:, 128 * n : 128 * n + 128]


def factor_kernel(rows_total, place_ref, own_ref, other_ref, high_ref, low_ref, work_ref):
    size = high_ref.shape[0]
    side = size // 2
    own, other = own_ref[...] / rows_total, other_ref[...] / rows_total
    flip = core_of(place_ref) != 0
    upper, lower = jnp.where(flip, other, own), jnp.where(flip, own, other)
    left = jnp.concatenate([upper[side:], lower[side:]], axis=0)
    work_ref[:side, :side] = upper[:side]
    work_ref[:side, side:size] = left.T
    work_ref[side:, :side] = left
    work_ref[side:, side:size] = lower[:side]
    at_row = lax.broadcasted_iota(jnp.int32, (size, size), 0)
    at_column = lax.broadcasted_iota(jnp.int32, (size, size), 1)
    work_ref[:, size:] = (at_row == at_column).astype(F32)
    inverse_factor(work_ref)
    at_row = lax.broadcasted_iota(jnp.int32, (size, size), 0)
    at_column = lax.broadcasted_iota(jnp.int32, (size, size), 1)
    high_ref[...], low_ref[...] = halves(jnp.where(at_row >= at_column, work_ref[:, size:], 0.0))


def apply_kernel(place_ref, ihigh_ref, ilow_ref, *refs):
    out_hbm, out_ref, sems = refs[-3:]
    parts = refs[:-3]
    ihigh, ilow = ihigh_ref[...], ilow_ref[...]
    writes = []
    for behind, part_ref in enumerate(parts):
        count = part_ref.shape[0]
        high, low = halves(part_ref[...])
        out_ref[behind] = mm(high, ihigh, NT) + (mm(high, ilow, NT) + mm(low, ihigh, NT))
        at = (y_of(place_ref) + len(parts) - behind) % len(parts) * count
        here = pl.ds(pl.multiple_of(at, count), count)
        writes.append(pltpu.make_async_copy(out_ref.at[behind], out_hbm.at[here, :], sems.at[behind]))
        writes[-1].start()
    for write in writes:
        write.wait()


def everyone(value, axes):
    return lax.all_to_all(value, axes, 0, 0)


def ahead(value, axis, steps):
    size = lax.axis_size(axis)
    return lax.ppermute(value, axis, [(at, (at + steps) % size) for at in range(size)])


def gather(value, axis):
    return [value] + [ahead(value, axis, steps) for steps in range(1, lax.axis_size(axis))]


def trade(parts, axis):
    return parts[:1] + [ahead(part, axis, steps) for steps, part in enumerate(parts) if steps]


def swap(value):
    return lax.ppermute(value, "core", [(0, 1), (1, 0)])


def total(values):
    first, second, third, fourth = values
    return (first + third) + (second + fourth)


def invert(place, own, other, columns, rows_total):
    return call(
        functools.partial(factor_kernel, rows_total),
        (jax.ShapeDtypeStruct((columns, columns), BF16),) * 2,
        in_specs=[SMEM_SPEC] + [VMEM_SPEC] * 2,
        scratch_shapes=[pltpu.VMEM((columns, 2 * columns), F32)],
    )(place, own, other)


def finish(place, inverse, blocks):
    count, columns = blocks[0].shape
    number = len(blocks)
    return call(
        apply_kernel,
        jax.ShapeDtypeStruct((number * count, columns), F32),
        in_specs=[SMEM_SPEC] + [VMEM_SPEC] * (2 + number),
        out_specs=pl.BlockSpec(memory_space=pltpu.HBM),
        scratch_shapes=[
            pltpu.VMEM((number, count, columns), F32),
            pltpu.SemaphoreType.DMA((number,)),
        ],
    )(place, *inverse, *blocks)


def on_device(tensor, context, offset, target):
    rows, width = tensor.shape[1:]
    ranks, columns = offset.shape[1], target.shape[1]
    nx, ny, nz = lax.axis_size("x"), lax.axis_size("y"), lax.axis_size(RING)
    place = pack_place(lax.axis_index("x"), lax.axis_index("y"), lax.axis_index("core"))

    high, low, product, given = project(place, offset, target, tensor)

    received = swap(given)
    parts = trade([product[n] + received[n] for n in range(nx)], "x")
    part = call(weights_kernel, jax.ShapeDtypeStruct((columns, context.shape[1]), F32))(*parts, context)
    size = ny * nz
    part = everyone(part.reshape(size, columns // size, -1), GROUP)
    part = call(sum_and_copy_kernel, jax.ShapeDtypeStruct(part.shape, F32))(part)
    weights = everyone(part, GROUP).reshape(columns, -1)
    expanded = call(expand_kernel, jax.ShapeDtypeStruct((width, columns), F32))(weights, context)
    behind = gather(expanded, "x")
    own = jnp.concatenate([behind[-n % nx] for n in range(nx)], axis=0)
    basis = make_basis(place, high, low, own, swap(own), ny)

    basis = total(trade(basis, "y"))
    basis = everyone(basis.reshape(nz, rows // ny // nz, columns), RING)
    basis = call(sum_and_copy_kernel, jax.ShapeDtypeStruct(basis.shape, F32))(basis)
    basis = everyone(basis, RING).reshape(rows // ny, columns)

    gram = call(
        gram_kernel,
        jax.ShapeDtypeStruct((2, 3 * columns // 4, columns // 2), F32),
        in_specs=[SMEM_SPEC, VMEM_SPEC],
    )(place, basis)
    mine = total(gather(gram[0] + swap(gram[1]), "y"))
    basis, mine = lax.optimization_barrier((basis, mine))
    blocks = gather(basis, "y")
    mine = total(gather(mine, "x"))
    inverse = invert(place, mine, swap(mine), columns, rows * lax.axis_size(TARGET))
    return finish(place, inverse, blocks)


def solution(mesh):
    fine = Mesh(mesh.devices.reshape(4, 2, 4, 4, 2), ("x", "core") + GROUP)
    placed = (
        P("zhi", TARGET, ("zlo", "y")),
        P(("zlo", "y"), None),
        P("zhi", None),
        P(TARGET, None),
    )
    return jax.shard_map(
        on_device, mesh=fine, in_specs=placed, out_specs=P(TARGET, None), check_vma=False
    )
```

```python
import functools

import jax
import jax.numpy as jnp
from jax import lax
from jax.experimental import pallas as pl
from jax.experimental.pallas import tpu as pltpu
from jax.sharding import Mesh
from jax.sharding import PartitionSpec as P

F32, BF16 = jnp.float32, jnp.bfloat16
TARGET = ("x", "core")
GROUP = ("zlo", "y", "zhi")
RING = ("zhi", "zlo")
ROWS_AT_ONCE = 256
NN = (((1,), (0,)), ((), ()))
TN = (((0,), (0,)), ((), ()))
NT = (((1,), (1,)), ((), ()))


def mm(a, b, dims=NN):
    return lax.dot_general(a, b, dims, preferred_element_type=F32)


def halves(value):
    high = value.astype(BF16)
    return high, (value - high.astype(F32)).astype(BF16)


def thirds(value):
    high = value.astype(BF16)
    rest = value - high.astype(F32)
    middle = rest.astype(BF16)
    return high, middle, (rest - middle.astype(F32)).astype(BF16)


def pack_place(x, y, core):
    return (8 * x + 2 * y + core).astype(jnp.int32).reshape(1)


def core_of(place_ref):
    return place_ref[0] & 1


def y_of(place_ref):
    return (place_ref[0] >> 1) & 3


def x_of(place_ref):
    return place_ref[0] >> 3


VMEM_SPEC = pl.BlockSpec(memory_space=pltpu.VMEM)
SMEM_SPEC = pl.BlockSpec(memory_space=pltpu.SMEM)


def in_hbm(value):
    return pltpu.with_memory_space_constraint(value, pltpu.HBM)


def in_vmem(value):
    return pltpu.with_memory_space_constraint(value, pltpu.VMEM)


def call(kernel, out_shape, vmem=16, **more):
    return pl.pallas_call(
        kernel,
        out_shape=out_shape,
        compiler_params=pltpu.CompilerParams(vmem_limit_bytes=vmem * 2**20),
        **more,
    )


def project_kernel(
    place_ref,
    offset_hbm,
    target_hbm,
    tensor_ref,
    high_ref,
    low_hbm,
    own_ref,
    near_ref,
    rest_ref,
    low_ref,
    held_ref,
    offset_ref,
    target_ref,
    factor_ref,
    sems,
):
    offsets, rows, width = tensor_ref.shape
    ranks = offset_ref.shape[0]
    blocks = held_ref.shape[0]
    depth = held_ref.shape[2]
    small = [
        pltpu.make_async_copy(offset_hbm, offset_ref, sems.at[blocks]),
        pltpu.make_async_copy(target_hbm, target_ref, sems.at[blocks + 1]),
    ]
    for copy in small:
        copy.start()
    for block in range(blocks):
        pltpu.make_async_copy(
            tensor_ref.at[:, pl.ds(block * depth, depth), :], held_ref.at[block], sems.at[block]
        ).start()
    for copy in small:
        copy.wait()

    def iota(shape, dim):
        return lax.broadcasted_iota(jnp.int32, shape, dim)

    tall, wide = (ranks * 16, ranks), (offsets, offsets * 16)
    at = iota(tall, 0) // 16
    half = ranks // 2
    core = jnp.where(at >= half, 1 - core_of(place_ref), core_of(place_ref))
    rank_at = 2 * ((at + x_of(place_ref)) % half) + core
    pick = (rank_at == iota(tall, 1)).astype(BF16)
    repeat = (iota(wide, 0) == iota(wide, 1) // 16).astype(BF16)
    spread = mm(mm(pick, offset_ref[...]).astype(BF16), repeat)
    same = iota(spread.shape, 0) % 16 == iota(spread.shape, 1) % 16
    spread = jnp.where(same, spread, 0.0).astype(BF16)
    factor_ref[...] = target_ref[...].astype(F32).T.astype(BF16)

    def contract(block):
        base = block * depth
        for at in range(0, depth, 32):
            sides = [
                held_ref[block, :, at + side : at + side + 16, :].reshape(-1, width) for side in (0, 16)
            ]
            high, low = halves(mm(spread, jnp.concatenate(sides, axis=1)))
            for rank in range(ranks):
                to = slice(rank * width, (rank + 1) * width)
                of = slice(rank * 16, rank * 16 + 16)
                for side in (0, 1):
                    rows_at = slice(base + at + 16 * side, base + at + 16 * side + 16)
                    lanes = slice(side * width, (side + 1) * width)
                    high_ref[rows_at, to] = high[of, lanes]
                    low_ref[rows_at, to] = low[of, lanes]

    def add_product(block):
        here = slice(block * depth, (block + 1) * depth)
        factor = factor_ref[:, here]
        for rank in range(0, ranks, 2):
            to = slice(rank * width, (rank + 2) * width)
            change = mm(factor, high_ref[here, to]) + mm(factor, low_ref[here, to])
            for side in (0, 1):
                part = change[:, side * width : (side + 1) * width]
                out_ref, of = own_ref, rank + side
                if rank >= half:
                    out_ref, of = (near_ref if side else rest_ref), (rank - half) // 2
                out_ref[of] = part if block == 0 else out_ref[of] + part

    def keep(block):
        here = pl.ds(block * depth, depth)
        return pltpu.make_async_copy(low_ref.at[here, :], low_hbm.at[here, :], sems.at[blocks + 2 + block])

    for block in range(blocks):
        pltpu.make_async_copy(
            tensor_ref.at[:, pl.ds(block * depth, depth), :], held_ref.at[block], sems.at[block]
        ).wait()
        contract(block)
        if block > 0:
            add_product(block - 1)
        keep(block).start()
    add_product(blocks - 1)
    for block in range(blocks):
        keep(block).wait()


def project(place, offset, target, tensor):
    offsets, rows, width = tensor.shape
    ranks, columns = offset.shape[1], target.shape[1]
    wide = ranks * width
    blocks = rows // ROWS_AT_ONCE
    return call(
        project_kernel,
        (
            jax.ShapeDtypeStruct((rows, wide), BF16),
            pltpu.HBM((rows, wide), BF16),
        )
        + tuple(jax.ShapeDtypeStruct((n, columns, width), F32) for n in (ranks // 2, ranks // 4, ranks // 4)),
        vmem=24,
        in_specs=[
            SMEM_SPEC,
        ]
        + [pl.BlockSpec(memory_space=pltpu.HBM)] * 3,
        out_specs=(VMEM_SPEC, pl.BlockSpec(memory_space=pltpu.HBM)) + (VMEM_SPEC,) * 3,
        scratch_shapes=[
            pltpu.VMEM((rows, wide), BF16),
            pltpu.VMEM((blocks, offsets, ROWS_AT_ONCE, width), BF16),
            pltpu.VMEM((ranks, offsets), BF16),
            pltpu.VMEM((rows, columns), BF16),
            pltpu.VMEM((columns, rows), BF16),
            pltpu.SemaphoreType.DMA((2 * blocks + 2,)),
        ],
    )(place, in_hbm(offset.T), in_hbm(target), in_hbm(tensor))


def weights_kernel(first_ref, second_ref, third_ref, fourth_ref, context_ref, out_ref):
    total = (first_ref[...] + second_ref[...]) + (third_ref[...] + fourth_ref[...])
    high, low = halves(total)
    context = context_ref[...]
    out_ref[...] = mm(high, context) + mm(low, context)


def sum_and_copy_kernel(parts_ref, out_ref):
    out_ref[...] = jnp.broadcast_to(jnp.sum(parts_ref[...], axis=0)[None], out_ref.shape)


def expand_kernel(weights_ref, context_ref, out_ref):
    high, low = halves(weights_ref[...])
    context = context_ref[...]
    out_ref[...] = mm(context, high, NT) + mm(context, low, NT)


def basis_kernel(high_ref, low_ref, value_ref, out_ref):
    vhigh, vlow = halves(value_ref[...])
    to = slice(0, value_ref.shape[0])
    for at in range(0, out_ref.shape[0], ROWS_AT_ONCE):
        rows = slice(at, at + ROWS_AT_ONCE)
        high = high_ref[rows, to]
        out_ref[rows, :] = mm(high, vhigh) + (mm(high, vlow) + mm(low_ref[rows, to], vhigh))


def rest_kernel(steps, blocks, place_ref, high_ref, low_ref, value_ref, sofar_ref, *out_refs):
    vhigh, vlow = halves(value_ref[...])
    depth = value_ref.shape[0]
    to = slice(depth, 2 * depth)
    for step, out_ref in zip(steps, out_refs):
        count = out_ref.shape[0]
        rows = pl.ds(pl.multiple_of((y_of(place_ref) + step) % blocks * count, count), count)
        high = high_ref[rows, to]
        total = mm(high, vhigh) + (mm(high, vlow) + mm(low_ref[rows, to], vhigh))
        out_ref[...] = sofar_ref[rows, :] + total


def make_basis(place, high, low, own, other, blocks):
    high, low = in_vmem(high), in_vmem(low)
    rows, columns = high.shape[0], own.shape[1]
    part = call(basis_kernel, jax.ShapeDtypeStruct((rows, columns), F32))(high, low, own)
    out = {}
    far = blocks // 2
    for steps in ((far,), tuple(step for step in range(blocks) if step != far)):
        values = call(
            functools.partial(rest_kernel, steps, blocks),
            (jax.ShapeDtypeStruct((rows // blocks, columns), F32),) * len(steps),
            in_specs=[SMEM_SPEC] + [VMEM_SPEC] * 4,
        )(place, high, low, other, part)
        out.update(zip(steps, values))
    return [out[step] for step in range(blocks)]


def gram_kernel(place_ref, basis_ref, out_ref):
    high, low = halves(basis_ref[...])
    cross = mm(high, low, TN)
    gram = mm(high, high, TN) + (cross + cross.T)
    side = gram.shape[0] // 2
    left, middle = gram[side:, :side], side // 2
    shares = [
        jnp.concatenate([gram[:side, :side], left[:middle]], axis=0),
        jnp.concatenate([gram[side:, side:], left[middle:]], axis=0),
    ]
    flip = core_of(place_ref) != 0
    out_ref[0] = jnp.where(flip, shares[1], shares[0])
    out_ref[1] = jnp.where(flip, shares[0], shares[1])


def row(value, at):
    return jnp.broadcast_to(value[at : at + 1, :], value.shape)


def small_inverse(columns):
    left = {(i, k): row(columns[k], i) for k in range(8) for i in range(k, 8)}
    unit, inverse = {}, {}
    for j in range(8):
        root = lax.rsqrt(left[j, j])
        square = root * root
        inverse[j, j] = root
        for k in range(j):
            inverse[j, k] = root * unit[j, k]
        for k in range(j + 1, 8):
            for i in range(k, 8):
                left[i, k] = left[i, k] - (left[i, j] * left[k, j]) * square
        for i in range(j + 1, 8):
            ratio = left[i, j] * square
            for k in range(j):
                unit[i, k] = unit[i, k] - ratio * unit[j, k]
            unit[i, j] = -ratio
    return inverse


def inverse_factor(work_ref):
    size, shape = work_ref.shape[0], (8, 128)
    at_row = lax.broadcasted_iota(jnp.int32, shape, 0)
    for top in range(0, size, 32):
        tiles = list(range(top // 128, size // 128))
        tiles += [size // 128 + t for t in range(top // 128 + 1)]
        rows = [
            {t: work_ref[top + 8 * q : top + 8 * q + 8, 128 * t : 128 * t + 128] for t in tiles}
            for q in range(4)
        ]
        columns = {}
        for q in range(4):
            for k in range(8 * (q + 1)):
                tile, lane = (top + k) // 128, (top + k) % 128
                columns[q, k] = jnp.broadcast_to(rows[q][tile][:, lane : lane + 1], shape)
        for q in range(4):
            inverse = small_inverse([columns[q, 8 * q + k] for k in range(8)])
            factor = {
                (o, j): sum(inverse[j, k] * columns[o, 8 * q + k] for k in range(j + 1))
                for o in range(q + 1, 4)
                for j in range(8)
            }
            for p in range(q + 1, 4):
                for k in range(8):
                    ratios = [row(factor[p, j], k) for j in range(8)]
                    for o in range(p, 4):
                        columns[o, 8 * p + k] -= sum(factor[o, j] * ratios[j] for j in range(8))
            spread = []
            for k in range(8):
                value = jnp.zeros(shape, F32)
                for i in range(k, 8):
                    value = jnp.where(at_row == i, inverse[i, k], value)
                spread.append(value)
            for t in tiles:
                mine = sum(spread[k] * row(rows[q][t], k) for k in range(8))
                rows[q][t] = mine
                for o in range(q + 1, 4):
                    rows[o][t] = rows[o][t] - sum(factor[o, j] * row(mine, j) for j in range(8))
        for q in range(4):
            for t in tiles:
                work_ref[top + 8 * q : top + 8 * q + 8, 128 * t : 128 * t + 128] = rows[q][t]
        below = top + 32
        if below < size:
            done = jnp.concatenate(
                [jnp.concatenate([rows[q][t] for q in range(4)], axis=0) for t in tiles], axis=1
            )
            high, middle, low = thirds(done)
            left = jnp.concatenate([high, high, middle, high, low, middle], axis=0)
            right = jnp.concatenate([high, middle, high, low, high, middle], axis=0)
            start, skip = 128 * tiles[0], below % 128
            change = mm(left[:, below - skip - start : size - start], right, TN)
            for n, t in enumerate(tiles):
                work_ref[below:, 128 * t : 128 * t + 128] -= change[skip:, 128 * n : 128 * n + 128]


def factor_kernel(rows_total, place_ref, own_ref, other_ref, high_ref, low_ref, work_ref):
    size = high_ref.shape[0]
    side = size // 2
    own, other = own_ref[...] / rows_total, other_ref[...] / rows_total
    flip = core_of(place_ref) != 0
    upper, lower = jnp.where(flip, other, own), jnp.where(flip, own, other)
    left = jnp.concatenate([upper[side:], lower[side:]], axis=0)
    work_ref[:side, :side] = upper[:side]
    work_ref[:side, side:size] = left.T
    work_ref[side:, :side] = left
    work_ref[side:, side:size] = lower[:side]
    at_row = lax.broadcasted_iota(jnp.int32, (size, size), 0)
    at_column = lax.broadcasted_iota(jnp.int32, (size, size), 1)
    work_ref[:, size:] = (at_row == at_column).astype(F32)
    inverse_factor(work_ref)
    at_row = lax.broadcasted_iota(jnp.int32, (size, size), 0)
    at_column = lax.broadcasted_iota(jnp.int32, (size, size), 1)
    high_ref[...], low_ref[...] = halves(jnp.where(at_row >= at_column, work_ref[:, size:], 0.0))


def apply_kernel(place_ref, ihigh_ref, ilow_ref, *refs):
    out_hbm, out_ref, sems = refs[-3:]
    parts = refs[:-3]
    ihigh, ilow = ihigh_ref[...], ilow_ref[...]
    writes = []
    for behind, part_ref in enumerate(parts):
        count = part_ref.shape[0]
        high, low = halves(part_ref[...])
        out_ref[behind] = mm(high, ihigh, NT) + (mm(high, ilow, NT) + mm(low, ihigh, NT))
        at = (y_of(place_ref) + len(parts) - behind) % len(parts) * count
        here = pl.ds(pl.multiple_of(at, count), count)
        writes.append(pltpu.make_async_copy(out_ref.at[behind], out_hbm.at[here, :], sems.at[behind]))
        writes[-1].start()
    for write in writes:
        write.wait()


def everyone(value, axes):
    return lax.all_to_all(value, axes, 0, 0)


def ahead(value, axis, steps):
    size = lax.axis_size(axis)
    return lax.ppermute(value, axis, [(at, (at + steps) % size) for at in range(size)])


def gather(value, axis):
    return [value] + [ahead(value, axis, steps) for steps in range(1, lax.axis_size(axis))]


def trade(parts, axis):
    return parts[:1] + [ahead(part, axis, steps) for steps, part in enumerate(parts) if steps]


def swap(value):
    return lax.ppermute(value, "core", [(0, 1), (1, 0)])


def total(values):
    first, second, third, fourth = values
    return (first + third) + (second + fourth)


def invert(place, own, other, columns, rows_total):
    return call(
        functools.partial(factor_kernel, rows_total),
        (jax.ShapeDtypeStruct((columns, columns), BF16),) * 2,
        in_specs=[SMEM_SPEC] + [VMEM_SPEC] * 2,
        scratch_shapes=[pltpu.VMEM((columns, 2 * columns), F32)],
    )(place, own, other)


def finish(place, inverse, blocks):
    count, columns = blocks[0].shape
    number = len(blocks)
    return call(
        apply_kernel,
        jax.ShapeDtypeStruct((number * count, columns), F32),
        in_specs=[SMEM_SPEC] + [VMEM_SPEC] * (2 + number),
        out_specs=pl.BlockSpec(memory_space=pltpu.HBM),
        scratch_shapes=[
            pltpu.VMEM((number, count, columns), F32),
            pltpu.SemaphoreType.DMA((number,)),
        ],
    )(place, *inverse, *blocks)


def on_device(tensor, context, offset, target):
    rows, width = tensor.shape[1:]
    ranks, columns = offset.shape[1], target.shape[1]
    nx, ny, nz = lax.axis_size("x"), lax.axis_size("y"), lax.axis_size(RING)
    place = pack_place(lax.axis_index("x"), lax.axis_index("y"), lax.axis_index("core"))

    high, low, product, near, rest = project(place, offset, target, tensor)

    near, rest = swap(near), swap(rest)
    parts = [product[n] + (near if n % 2 else rest)[n // 2] for n in range(nx)]
    parts = trade(parts, "x")
    part = call(weights_kernel, jax.ShapeDtypeStruct((columns, context.shape[1]), F32))(*parts, context)
    size = ny * nz
    part = everyone(part.reshape(size, columns // size, -1), GROUP)
    part = call(sum_and_copy_kernel, jax.ShapeDtypeStruct(part.shape, F32))(part)
    weights = everyone(part, GROUP).reshape(columns, -1)
    expanded = call(expand_kernel, jax.ShapeDtypeStruct((width, columns), F32))(weights, context)
    behind = gather(expanded, "x")
    own = jnp.concatenate([behind[-n % nx] for n in range(nx)], axis=0)
    basis = make_basis(place, high, low, own, swap(own), ny)

    basis = total(trade(basis, "y"))
    basis = everyone(basis.reshape(nz, rows // ny // nz, columns), RING)
    basis = call(sum_and_copy_kernel, jax.ShapeDtypeStruct(basis.shape, F32))(basis)
    basis = everyone(basis, RING).reshape(rows // ny, columns)

    gram = call(
        gram_kernel,
        jax.ShapeDtypeStruct((2, 3 * columns // 4, columns // 2), F32),
        in_specs=[SMEM_SPEC, VMEM_SPEC],
    )(place, basis)
    mine = total(gather(gram[0] + swap(gram[1]), "y"))
    basis, mine = lax.optimization_barrier((basis, mine))
    blocks = gather(basis, "y")
    mine = total(gather(mine, "x"))
    inverse = invert(place, mine, swap(mine), columns, rows * lax.axis_size(TARGET))
    return finish(place, inverse, blocks)


def solution(mesh):
    fine = Mesh(mesh.devices.reshape(4, 2, 4, 4, 2), ("x", "core") + GROUP)
    placed = (
        P("zhi", TARGET, ("zlo", "y")),
        P(("zlo", "y"), None),
        P("zhi", None),
        P(TARGET, None),
    )
    return jax.shard_map(
        on_device, mesh=fine, in_specs=placed, out_specs=P(TARGET, None), check_vma=False
    )
```

```python
import functools

import jax
import jax.numpy as jnp
from jax import lax
from jax.experimental import pallas as pl
from jax.experimental.pallas import tpu as pltpu
from jax.sharding import Mesh
from jax.sharding import PartitionSpec as P

F32, BF16 = jnp.float32, jnp.bfloat16
TARGET = ("x", "core")
GROUP = ("zlo", "y", "zhi")
RING = ("zhi", "zlo")
ROWS_AT_ONCE = 256
NN = (((1,), (0,)), ((), ()))
TN = (((0,), (0,)), ((), ()))
NT = (((1,), (1,)), ((), ()))


def mm(a, b, dims=NN):
    return lax.dot_general(a, b, dims, preferred_element_type=F32)


def halves(value):
    high = value.astype(BF16)
    return high, (value - high.astype(F32)).astype(BF16)


def thirds(value):
    high = value.astype(BF16)
    rest = value - high.astype(F32)
    middle = rest.astype(BF16)
    return high, middle, (rest - middle.astype(F32)).astype(BF16)


def pack_place(x, y, core):
    return (8 * x + 2 * y + core).astype(jnp.int32).reshape(1)


def core_of(place_ref):
    return place_ref[0] & 1


def y_of(place_ref):
    return (place_ref[0] >> 1) & 3


def x_of(place_ref):
    return place_ref[0] >> 3


VMEM_SPEC = pl.BlockSpec(memory_space=pltpu.VMEM)
SMEM_SPEC = pl.BlockSpec(memory_space=pltpu.SMEM)


def in_hbm(value):
    return pltpu.with_memory_space_constraint(value, pltpu.HBM)


def in_vmem(value):
    return pltpu.with_memory_space_constraint(value, pltpu.VMEM)


def call(kernel, out_shape, vmem=16, **more):
    return pl.pallas_call(
        kernel,
        out_shape=out_shape,
        compiler_params=pltpu.CompilerParams(vmem_limit_bytes=vmem * 2**20),
        **more,
    )


def project_kernel(
    place_ref,
    offset_hbm,
    target_hbm,
    tensor_ref,
    high_ref,
    low_hbm,
    own_ref,
    near_ref,
    rest_ref,
    low_ref,
    held_ref,
    offset_ref,
    target_ref,
    factor_ref,
    sems,
):
    offsets, rows, width = tensor_ref.shape
    ranks = offset_ref.shape[0]
    blocks = held_ref.shape[0]
    depth = held_ref.shape[2]
    small = [
        pltpu.make_async_copy(offset_hbm, offset_ref, sems.at[blocks]),
        pltpu.make_async_copy(target_hbm, target_ref, sems.at[blocks + 1]),
    ]
    for copy in small:
        copy.start()
    for block in range(blocks):
        pltpu.make_async_copy(
            tensor_ref.at[:, pl.ds(block * depth, depth), :], held_ref.at[block], sems.at[block]
        ).start()
    for copy in small:
        copy.wait()

    def iota(shape, dim):
        return lax.broadcasted_iota(jnp.int32, shape, dim)

    tall, wide = (ranks * 16, ranks), (offsets, offsets * 16)
    at = iota(tall, 0) // 16
    half = ranks // 2
    core = jnp.where(at >= half, 1 - core_of(place_ref), core_of(place_ref))
    rank_at = 2 * ((at + x_of(place_ref)) % half) + core
    pick = (rank_at == iota(tall, 1)).astype(BF16)
    repeat = (iota(wide, 0) == iota(wide, 1) // 16).astype(BF16)
    spread = mm(mm(pick, offset_ref[...]).astype(BF16), repeat)
    same = iota(spread.shape, 0) % 16 == iota(spread.shape, 1) % 16
    spread = jnp.where(same, spread, 0.0).astype(BF16)
    factor_ref[...] = target_ref[...].astype(F32).T.astype(BF16)

    def contract(block):
        base = block * depth
        for at in range(0, depth, 32):
            sides = [
                held_ref[block, :, at + side : at + side + 16, :].reshape(-1, width) for side in (0, 16)
            ]
            high, low = halves(mm(spread, jnp.concatenate(sides, axis=1)))
            for rank in range(ranks):
                to = slice(rank * width, (rank + 1) * width)
                of = slice(rank * 16, rank * 16 + 16)
                for side in (0, 1):
                    rows_at = slice(base + at + 16 * side, base + at + 16 * side + 16)
                    lanes = slice(side * width, (side + 1) * width)
                    high_ref[rows_at, to] = high[of, lanes]
                    low_ref[rows_at, to] = low[of, lanes]

    def add_product(block):
        here = slice(block * depth, (block + 1) * depth)
        factor = factor_ref[:, here]
        for rank in range(0, ranks, 2):
            to = slice(rank * width, (rank + 2) * width)
            change = mm(factor, high_ref[here, to]) + mm(factor, low_ref[here, to])
            for side in (0, 1):
                part = change[:, side * width : (side + 1) * width]
                out_ref, of = own_ref, rank + side
                if rank >= half:
                    out_ref, of = (near_ref if side else rest_ref), (rank - half) // 2
                out_ref[of] = part if block == 0 else out_ref[of] + part

    def keep(block):
        here = pl.ds(block * depth, depth)
        return pltpu.make_async_copy(low_ref.at[here, :], low_hbm.at[here, :], sems.at[blocks + 2 + block])

    for block in range(blocks):
        pltpu.make_async_copy(
            tensor_ref.at[:, pl.ds(block * depth, depth), :], held_ref.at[block], sems.at[block]
        ).wait()
        contract(block)
        if block > 0:
            add_product(block - 1)
        keep(block).start()
    add_product(blocks - 1)
    for block in range(blocks):
        keep(block).wait()


def project(place, offset, target, tensor):
    offsets, rows, width = tensor.shape
    ranks, columns = offset.shape[1], target.shape[1]
    wide = ranks * width
    blocks = rows // ROWS_AT_ONCE
    return call(
        project_kernel,
        (
            jax.ShapeDtypeStruct((rows, wide), BF16),
            pltpu.HBM((rows, wide), BF16),
        )
        + tuple(jax.ShapeDtypeStruct((n, columns, width), F32) for n in (ranks // 2, ranks // 4, ranks // 4)),
        vmem=24,
        in_specs=[
            SMEM_SPEC,
        ]
        + [pl.BlockSpec(memory_space=pltpu.HBM)] * 3,
        out_specs=(VMEM_SPEC, pl.BlockSpec(memory_space=pltpu.HBM)) + (VMEM_SPEC,) * 3,
        scratch_shapes=[
            pltpu.VMEM((rows, wide), BF16),
            pltpu.VMEM((blocks, offsets, ROWS_AT_ONCE, width), BF16),
            pltpu.VMEM((ranks, offsets), BF16),
            pltpu.VMEM((rows, columns), BF16),
            pltpu.VMEM((columns, rows), BF16),
            pltpu.SemaphoreType.DMA((2 * blocks + 2,)),
        ],
    )(place, in_hbm(offset.T), in_hbm(target), in_hbm(tensor))


def weights_kernel(first_ref, second_ref, third_ref, fourth_ref, context_ref, out_ref):
    total = (first_ref[...] + second_ref[...]) + (third_ref[...] + fourth_ref[...])
    high, low = halves(total)
    context = context_ref[...]
    out_ref[...] = mm(high, context) + mm(low, context)


def sum_and_copy_kernel(parts_ref, out_ref):
    out_ref[...] = jnp.broadcast_to(jnp.sum(parts_ref[...], axis=0)[None], out_ref.shape)


def expand_kernel(weights_ref, context_ref, out_ref):
    high, low = halves(weights_ref[...])
    context = context_ref[...]
    out_ref[...] = mm(context, high, NT) + mm(context, low, NT)


def basis_kernel(high_ref, low_ref, value_ref, out_ref):
    vhigh, vlow = halves(value_ref[...])
    to = slice(0, value_ref.shape[0])
    for at in range(0, out_ref.shape[0], ROWS_AT_ONCE):
        rows = slice(at, at + ROWS_AT_ONCE)
        high = high_ref[rows, to]
        out_ref[rows, :] = mm(high, vhigh) + (mm(high, vlow) + mm(low_ref[rows, to], vhigh))


def rest_kernel(steps, blocks, place_ref, high_ref, low_ref, value_ref, sofar_ref, *out_refs):
    vhigh, vlow = halves(value_ref[...])
    depth = value_ref.shape[0]
    to = slice(depth, 2 * depth)
    for step, out_ref in zip(steps, out_refs):
        count = out_ref.shape[0]
        rows = pl.ds(pl.multiple_of((y_of(place_ref) + step) % blocks * count, count), count)
        high = high_ref[rows, to]
        total = mm(high, vhigh) + (mm(high, vlow) + mm(low_ref[rows, to], vhigh))
        out_ref[...] = sofar_ref[rows, :] + total


def make_basis(place, high, low, own, other, blocks):
    high, low = in_vmem(high), in_vmem(low)
    rows, columns = high.shape[0], own.shape[1]
    part = call(basis_kernel, jax.ShapeDtypeStruct((rows, columns), F32))(high, low, own)
    out = {}
    far = blocks // 2
    for steps in ((far,), tuple(step for step in range(blocks) if step != far)):
        values = call(
            functools.partial(rest_kernel, steps, blocks),
            (jax.ShapeDtypeStruct((rows // blocks, columns), F32),) * len(steps),
            in_specs=[SMEM_SPEC] + [VMEM_SPEC] * 4,
        )(place, high, low, other, part)
        out.update(zip(steps, values))
    return [out[step] for step in range(blocks)]


def gram_kernel(place_ref, basis_ref, out_ref):
    high, low = halves(basis_ref[...])
    cross = mm(high, low, TN)
    gram = mm(high, high, TN) + (cross + cross.T)
    side = gram.shape[0] // 2
    left, middle = gram[side:, :side], side // 2
    shares = [
        jnp.concatenate([gram[:side, :side], left[:middle]], axis=0),
        jnp.concatenate([gram[side:, side:], left[middle:]], axis=0),
    ]
    flip = core_of(place_ref) != 0
    out_ref[0] = jnp.where(flip, shares[1], shares[0])
    out_ref[1] = jnp.where(flip, shares[0], shares[1])


def row(value, at):
    return jnp.broadcast_to(value[at : at + 1, :], value.shape)


def small_inverse(columns):
    left = {(i, k): row(columns[k], i) for k in range(8) for i in range(k, 8)}
    unit, inverse = {}, {}
    for j in range(8):
        root = lax.rsqrt(left[j, j])
        square = root * root
        inverse[j, j] = root
        for k in range(j):
            inverse[j, k] = root * unit[j, k]
        for k in range(j + 1, 8):
            for i in range(k, 8):
                left[i, k] = left[i, k] - (left[i, j] * left[k, j]) * square
        for i in range(j + 1, 8):
            ratio = left[i, j] * square
            for k in range(j):
                unit[i, k] = unit[i, k] - ratio * unit[j, k]
            unit[i, j] = -ratio
    return inverse


def inverse_factor(work_ref):
    size, shape = work_ref.shape[0], (8, 128)
    at_row = lax.broadcasted_iota(jnp.int32, shape, 0)
    for top in range(0, size, 32):
        tiles = list(range(top // 128, size // 128))
        tiles += [size // 128 + t for t in range(top // 128 + 1)]
        rows = [
            {t: work_ref[top + 8 * q : top + 8 * q + 8, 128 * t : 128 * t + 128] for t in tiles}
            for q in range(4)
        ]
        columns = {}
        for q in range(4):
            for k in range(8 * (q + 1)):
                tile, lane = (top + k) // 128, (top + k) % 128
                columns[q, k] = jnp.broadcast_to(rows[q][tile][:, lane : lane + 1], shape)
        for q in range(4):
            inverse = small_inverse([columns[q, 8 * q + k] for k in range(8)])
            factor = {
                (o, j): sum(inverse[j, k] * columns[o, 8 * q + k] for k in range(j + 1))
                for o in range(q + 1, 4)
                for j in range(8)
            }
            for p in range(q + 1, 4):
                for k in range(8):
                    ratios = [row(factor[p, j], k) for j in range(8)]
                    for o in range(p, 4):
                        columns[o, 8 * p + k] -= sum(factor[o, j] * ratios[j] for j in range(8))
            spread = []
            for k in range(8):
                value = jnp.zeros(shape, F32)
                for i in range(k, 8):
                    value = jnp.where(at_row == i, inverse[i, k], value)
                spread.append(value)
            for t in tiles:
                mine = sum(spread[k] * row(rows[q][t], k) for k in range(8))
                rows[q][t] = mine
                for o in range(q + 1, 4):
                    rows[o][t] = rows[o][t] - sum(factor[o, j] * row(mine, j) for j in range(8))
        for q in range(4):
            for t in tiles:
                work_ref[top + 8 * q : top + 8 * q + 8, 128 * t : 128 * t + 128] = rows[q][t]
        below = top + 32
        if below < size:
            done = jnp.concatenate(
                [jnp.concatenate([rows[q][t] for q in range(4)], axis=0) for t in tiles], axis=1
            )
            high, middle, low = thirds(done)
            left = jnp.concatenate([high, high, middle, high, low, middle], axis=0)
            right = jnp.concatenate([high, middle, high, low, high, middle], axis=0)
            start, skip = 128 * tiles[0], below % 128
            change = mm(left[:, below - skip - start : size - start], right, TN)
            for n, t in enumerate(tiles):
                work_ref[below:, 128 * t : 128 * t + 128] -= change[skip:, 128 * n : 128 * n + 128]


def factor_kernel(rows_total, place_ref, own_ref, other_ref, high_ref, low_ref, work_ref):
    size = high_ref.shape[0]
    side = size // 2
    own, other = own_ref[...] / rows_total, other_ref[...] / rows_total
    flip = core_of(place_ref) != 0
    upper, lower = jnp.where(flip, other, own), jnp.where(flip, own, other)
    left = jnp.concatenate([upper[side:], lower[side:]], axis=0)
    work_ref[:side, :side] = upper[:side]
    work_ref[:side, side:size] = left.T
    work_ref[side:, :side] = left
    work_ref[side:, side:size] = lower[:side]
    at_row = lax.broadcasted_iota(jnp.int32, (size, size), 0)
    at_column = lax.broadcasted_iota(jnp.int32, (size, size), 1)
    work_ref[:, size:] = (at_row == at_column).astype(F32)
    inverse_factor(work_ref)
    at_row = lax.broadcasted_iota(jnp.int32, (size, size), 0)
    at_column = lax.broadcasted_iota(jnp.int32, (size, size), 1)
    high_ref[...], low_ref[...] = halves(jnp.where(at_row >= at_column, work_ref[:, size:], 0.0))


def apply_kernel(place_ref, ihigh_ref, ilow_ref, *refs):
    out_hbm, out_ref, sems = refs[-3:]
    parts = refs[:-3]
    ihigh, ilow = ihigh_ref[...], ilow_ref[...]
    writes = []
    for behind, part_ref in enumerate(parts):
        count = part_ref.shape[0]
        high, low = halves(part_ref[...])
        out_ref[behind] = mm(high, ihigh, NT) + (mm(high, ilow, NT) + mm(low, ihigh, NT))
        at = (y_of(place_ref) + len(parts) - behind) % len(parts) * count
        here = pl.ds(pl.multiple_of(at, count), count)
        writes.append(pltpu.make_async_copy(out_ref.at[behind], out_hbm.at[here, :], sems.at[behind]))
        writes[-1].start()
    for write in writes:
        write.wait()


def everyone(value, axes):
    return lax.all_to_all(value, axes, 0, 0)


def ahead(value, axis, steps):
    size = lax.axis_size(axis)
    return lax.ppermute(value, axis, [(at, (at + steps) % size) for at in range(size)])


def copy_kernel(value_ref, out_ref):
    out_ref[...] = value_ref[...]


def gather(value, axis, late=True):
    size = lax.axis_size(axis)
    again = call(copy_kernel, jax.ShapeDtypeStruct(value.shape, F32))(value) if late else value
    return [value] + [
        ahead(again if steps == size // 2 else value, axis, steps) for steps in range(1, size)
    ]


def trade(parts, axis):
    return parts[:1] + [ahead(part, axis, steps) for steps, part in enumerate(parts) if steps]


def swap(value):
    return lax.ppermute(value, "core", [(0, 1), (1, 0)])


def total(values):
    first, second, third, fourth = values
    return (first + third) + (second + fourth)


def invert(place, own, other, columns, rows_total):
    return call(
        functools.partial(factor_kernel, rows_total),
        (jax.ShapeDtypeStruct((columns, columns), BF16),) * 2,
        in_specs=[SMEM_SPEC] + [VMEM_SPEC] * 2,
        scratch_shapes=[pltpu.VMEM((columns, 2 * columns), F32)],
    )(place, own, other)


def finish(place, inverse, blocks):
    count, columns = blocks[0].shape
    number = len(blocks)
    return call(
        apply_kernel,
        jax.ShapeDtypeStruct((number * count, columns), F32),
        in_specs=[SMEM_SPEC] + [VMEM_SPEC] * (2 + number),
        out_specs=pl.BlockSpec(memory_space=pltpu.HBM),
        scratch_shapes=[
            pltpu.VMEM((number, count, columns), F32),
            pltpu.SemaphoreType.DMA((number,)),
        ],
    )(place, *inverse, *blocks)


def on_device(tensor, context, offset, target):
    rows, width = tensor.shape[1:]
    ranks, columns = offset.shape[1], target.shape[1]
    nx, ny, nz = lax.axis_size("x"), lax.axis_size("y"), lax.axis_size(RING)
    place = pack_place(lax.axis_index("x"), lax.axis_index("y"), lax.axis_index("core"))

    high, low, product, near, rest = project(place, offset, target, tensor)

    near, rest = swap(near), swap(rest)
    parts = [product[n] + (near if n % 2 else rest)[n // 2] for n in range(nx)]
    parts = trade(parts, "x")
    part = call(weights_kernel, jax.ShapeDtypeStruct((columns, context.shape[1]), F32))(*parts, context)
    size = ny * nz
    part = everyone(part.reshape(size, columns // size, -1), GROUP)
    part = call(sum_and_copy_kernel, jax.ShapeDtypeStruct(part.shape, F32))(part)
    weights = everyone(part, GROUP).reshape(columns, -1)
    expanded = call(expand_kernel, jax.ShapeDtypeStruct((width, columns), F32))(weights, context)
    behind = gather(expanded, "x")
    own = jnp.concatenate([behind[-n % nx] for n in range(nx)], axis=0)
    basis = make_basis(place, high, low, own, swap(own), ny)

    basis = total(trade(basis, "y"))
    basis = everyone(basis.reshape(nz, rows // ny // nz, columns), RING)
    basis = call(sum_and_copy_kernel, jax.ShapeDtypeStruct(basis.shape, F32))(basis)
    basis = everyone(basis, RING).reshape(rows // ny, columns)

    gram = call(
        gram_kernel,
        jax.ShapeDtypeStruct((2, 3 * columns // 4, columns // 2), F32),
        in_specs=[SMEM_SPEC, VMEM_SPEC],
    )(place, basis)
    mine = total(gather(gram[0] + swap(gram[1]), "y"))
    basis, mine = lax.optimization_barrier((basis, mine))
    blocks = gather(basis, "y", late=False)
    mine = total(gather(mine, "x"))
    inverse = invert(place, mine, swap(mine), columns, rows * lax.axis_size(TARGET))
    return finish(place, inverse, blocks)


def solution(mesh):
    fine = Mesh(mesh.devices.reshape(4, 2, 4, 4, 2), ("x", "core") + GROUP)
    placed = (
        P("zhi", TARGET, ("zlo", "y")),
        P(("zlo", "y"), None),
        P("zhi", None),
        P(TARGET, None),
    )
    return jax.shard_map(
        on_device, mesh=fine, in_specs=placed, out_specs=P(TARGET, None), check_vma=False
    )
```
